32 devices in a mesh: gx: 4 (over y, core), gy: 8 (over z, x).
Axes of the slice: x: 2, y: 2, z: 4, core: 2. Of those that a mesh axis runs over, the one named last changes fastest.
Arguments:
- flow_fields: float32 [6, 16, 256, 1024], P(None, None, 'gx', 'gy'), may hold values from -6 to 6
- cell_index: int32 [3, 32768], P(None, ('gx', 'gy')), may hold values from 0 to 127, as said below
- stencil_shift: int32 [3, 32768], P(None, ('gx', 'gy')), may hold values from -1 to 0
- fraction_in_cell: float32 [3, 32768], P(None, ('gx', 'gy')), may hold values from 0 to 1
- bubble_speed: float32 [3, 32768], P(None, ('gx', 'gy')), may hold values from -6 to 6
- history: float32 [3, 256, 32768], P(None, None, ('gx', 'gy')), may hold values from -4 to 4
- live_count: int32 [32], P(('gx', 'gy')), may hold values from 512 to 1024, as said below
- mig_slots: int32 [32, 8, 16], P(('gx', 'gy')), may hold values from 0 to 1023, as said below
- mig_count: int32 [32, 8], P(('gx', 'gy')), may hold values from 0 to 16, as said below
Outputs:
- new_speed: float32 [3, 32768], P(None, ('gx', 'gy'))
- new_position: float32 [3, 32768], P(None, ('gx', 'gy'))
- new_history: float32 [3, 256, 32768], P(None, None, ('gx', 'gy'))
- arrived_state: float32 [8, 6, 512], P(None, None, ('gx', 'gy'))
- arrived_history: float32 [8, 3, 256, 512], P(None, None, None, ('gx', 'gy'))
The draws below stay inside these ranges and needn't reach their ends.
Inputs may be any that keep to these rules, and one draw needn't show every extreme that they name: `cell_index`: each component lies in its tile: x below 64, y below 128, z below 16. `live_count`: at least half of 1024 and at least 128; some tile is full. `mig_slots`: the used entries of a tile's 8 lists are distinct live slots of that tile; entries past the count are slots too and are ignored. `mig_count`: some list is full in every draw.
All inputs are finite; a program needn't handle non-finite values.
Results may differ from the reference program's by a relative error of at most 0.0003.
Values sent between devices are 32-bit elements; how exact they have to be, the bound alone decides.
A program may use at most 192 MiB of HBM per device.

```python
import jax
import jax.numpy as jnp
from jax import lax

CX = 64
CY = 128
NZ = 16
NB = 1024
CAP = 16
H = 256
NX = 256
NY = 1024
TILES = 32
BUB = 32768
ARR = 512
N_GX = 4
N_GY = 8


def tile_loads(key):
    base = jax.random.fold_in(key, 4242)
    lowest = max(8 * CAP, NB // 2)
    live = jax.random.randint(jax.random.fold_in(base, 1), (TILES,), lowest, NB + 1, dtype=jnp.int32)
    full = jax.random.randint(jax.random.fold_in(base, 2), (), 0, TILES, dtype=jnp.int32)
    other = (full + 1 + jax.random.randint(jax.random.fold_in(base, 3), (), 0, TILES - 1, dtype=jnp.int32)) % TILES
    live = live.at[other].set(lowest)
    live = live.at[full].set(NB)
    return live


def draw_live_count(key, part):
    return tile_loads(key)


def draw_mig_slots(key, part):
    live = tile_loads(key)
    base = jax.random.fold_in(key, 777)

    def one_tile(tile, limit):
        perm = jax.random.permutation(jax.random.fold_in(base, tile), NB).astype(jnp.int32)
        order = jnp.argsort(jnp.where(perm < limit, 0, 1).astype(jnp.int32), stable=True)
        return perm[order][:8 * CAP].reshape(8, CAP)
    return jax.vmap(one_tile)(jnp.arange(TILES, dtype=jnp.int32), live)


def draw_mig_count(key, part):
    base = jax.random.fold_in(key, 913)
    counts = jax.random.randint(jax.random.fold_in(base, 1), (TILES * 8,), 0, CAP + 1, dtype=jnp.int32)
    spot = jax.random.randint(jax.random.fold_in(base, 2), (), 0, TILES * 8, dtype=jnp.int32)
    return counts.at[spot].set(CAP).reshape(TILES, 8)


def draw_cell_index(key, part):
    base = jax.random.fold_in(key, 31)
    cell_x = jax.random.randint(jax.random.fold_in(base, 1), (TILES * NB,), 0, CX, dtype=jnp.int32)
    cell_y = jax.random.randint(jax.random.fold_in(base, 2), (TILES * NB,), 0, CY, dtype=jnp.int32)
    cell_z = jax.random.randint(jax.random.fold_in(base, 3), (TILES * NB,), 0, NZ, dtype=jnp.int32)
    return jnp.stack([cell_x, cell_y, cell_z])


def plant(entries, key, low, high):
    longest = entries.shape.index(max(entries.shape))
    spots = []
    for shift in (0, 1):
        where = [jax.random.randint(jax.random.fold_in(key, axis), (), 0, length) for axis, length in enumerate(entries.shape)]
        where[longest] = (where[longest] + shift) % entries.shape[longest]
        spots.append(tuple(where))
    return entries.at[spots[0]].set(low).at[spots[1]].set(high)


def level_of(key, extent, shards, smallest, high):
    def one(dim, blocks):
        heights = jax.random.uniform(jax.random.fold_in(jax.random.fold_in(key, 6), dim), (blocks,), jnp.float32, smallest / len(shards), high / len(shards))
        return jnp.repeat(jnp.exp(heights), extent[dim] // blocks).reshape((-1,) + (1,) * (len(extent) - dim - 1))

    loudness = one(*shards[0])
    for cut in shards[1:]:
        loudness = loudness * one(*cut)
    return loudness


def scatter_about(own_key, extent, deviation, bound, pieces=(), kind=jnp.bfloat16):
    entries = deviation * jax.random.normal(own_key, extent, jnp.float32)
    if pieces:
        entries = entries * level_of(own_key, extent, pieces, -0.22, 0.18)
    return jnp.clip(entries, -bound, bound).astype(kind)


def setup_inputs(seed: int = 0) -> dict:
    key_of = jax.random.split(jax.random.key(seed), 10)
    return {
        "flow_fields": scatter_about(key_of[0], (6, NZ, NX, NY), 1.0, 6.0, ((2, 4), (3, 8)), jnp.float32),
        "cell_index": draw_cell_index(jax.random.fold_in(key_of[9], 71), 0),
        "stencil_shift": plant(jax.random.randint(key_of[2], (3, BUB), -1, 1), jax.random.fold_in(key_of[2], 1), -1, 0).astype(jnp.int32),
        "fraction_in_cell": jnp.clip(1.0 * jax.random.uniform(key_of[3], (3, BUB), jnp.float32) ** level_of(key_of[3], (3, BUB), ((1, 32),), -0.2, 0.2), 0.0, 1.0),
        "bubble_speed": scatter_about(key_of[4], (3, BUB), 1.0, 6.0, ((1, 32),), jnp.float32),
        "history": scatter_about(key_of[5], (3, H, BUB), 0.5, 4.0, ((2, 32),), jnp.float32),
        "live_count": draw_live_count(jax.random.fold_in(key_of[9], 71), 0),
        "mig_slots": draw_mig_slots(jax.random.fold_in(key_of[9], 71), 0),
        "mig_count": draw_mig_count(jax.random.fold_in(key_of[9], 71), 0),
    }


neighbours = ((-1, -1), (-1, 0), (-1, 1), (0, -1), (0, 1), (1, -1), (1, 0), (1, 1))
step_dt = 0.1
relax_tau = 0.5
basset_coef = 0.3

def lagrange_basis(s):
    return jnp.stack([-s * (s - 1.0) * (s - 2.0) / 6.0, (s + 1.0) * (s - 1.0) * (s - 2.0) / 2.0, -(s + 1.0) * s * (s - 2.0) / 2.0, (s + 1.0) * s * (s - 1.0) / 6.0])

def advance(fluid_field, speed, fraction_part, history, alive):
    steps_h = history.shape[1]
    karg = jnp.arange(1, steps_h + 1, dtype=jnp.float32)
    quad = jnp.sqrt(karg + 1.0) - jnp.sqrt(karg)
    tail = jnp.einsum('ckb,k->cb', history, quad, precision=lax.Precision.HIGHEST)
    fluid_u = fluid_field[0:3]
    fluid_a = fluid_field[3:6]

    def rate(v):
        return 3.0 * fluid_a + (fluid_u - v) / relax_tau + basset_coef * (fluid_u - v + tail)
    v1 = speed + step_dt * rate(speed)
    v2 = 0.75 * speed + 0.25 * (v1 + step_dt * rate(v1))
    vn = speed / 3.0 + 2.0 / 3.0 * (v2 + step_dt * rate(v2))
    posn = fraction_part + step_dt * (speed / 6.0 + v1 / 6.0 + 2.0 * v2 / 3.0)
    hist_new = jnp.concatenate([(fluid_u - vn)[:, None, :], history[:, :steps_h - 1, :]], axis=1)
    keep = alive.astype(jnp.float32)
    return (vn * keep, posn * keep, hist_new * keep)

def reference(flow_fields, cell_index, stencil_shift, fraction_in_cell, bubble_speed, history, live_count, mig_slots, mig_count):
    flow_flat = flow_fields.reshape(6, NZ * NX * NY)
    nodes = jnp.arange(-1, 3, dtype=jnp.int32)

    def per_tile(inputs):
        tile, cells, offset_values, fraction_part, speed, hist, live, slots, counts = inputs
        row_i = tile // N_GY
        row_j = tile % N_GY
        bx = row_i * CX + cells[0] + offset_values[0]
        by = row_j * CY + cells[1] + offset_values[1]
        bz = cells[2] + offset_values[2]
        xs = (bx[None, :] + nodes[:, None]) % NX
        ys = (by[None, :] + nodes[:, None]) % NY
        zs = (bz[None, :] + nodes[:, None]) % NZ
        sampled_value = fraction_part - offset_values.astype(jnp.float32)
        weight_along_x = lagrange_basis(sampled_value[0])
        weight_along_y = lagrange_basis(sampled_value[1])
        weight_along_z = lagrange_basis(sampled_value[2])
        idx = (zs[:, None, None, :] * (NX * NY) + xs[None, :, None, :] * NY + ys[None, None, :, :]).reshape(64, -1)
        combined_weight = (weight_along_z[:, None, None, :] * weight_along_x[None, :, None, :] * weight_along_y[None, None, :, :]).reshape(64, -1)
        selected_samples = flow_flat[:, idx]
        fluid_field = jnp.einsum('rey,ey->ry', selected_samples, combined_weight, precision=lax.Precision.HIGHEST)
        alive = jnp.arange(NB, dtype=jnp.int32) < live
        vn, posn, hist_new = advance(fluid_field, speed, fraction_part, hist, alive)
        state = jnp.concatenate([vn, posn], axis=0)
        used = (jnp.arange(CAP, dtype=jnp.int32)[None, :] < counts[:, None]).astype(jnp.float32)
        out_state = jnp.transpose(state[:, slots], (1, 0, 2)) * used[:, None, :]
        out_hist = jnp.transpose(hist_new[:, :, slots], (2, 0, 1, 3)) * used[:, None, None, :]
        return (vn, posn, hist_new, out_state, out_hist)

    def tiles_first(a):
        return jnp.moveaxis(a.reshape(a.shape[:-1] + (TILES, NB)), -2, 0)
    tile_ids = jnp.arange(TILES, dtype=jnp.int32)
    vn, posn, hist_new, out_state, out_hist = lax.map(per_tile, (tile_ids, tiles_first(cell_index), tiles_first(stencil_shift), tiles_first(fraction_in_cell), tiles_first(bubble_speed), tiles_first(history), live_count, mig_slots, mig_count))
    new_speed = jnp.transpose(vn, (1, 0, 2)).reshape(3, BUB)
    new_position = jnp.transpose(posn, (1, 0, 2)).reshape(3, BUB)
    new_history = jnp.transpose(hist_new, (1, 2, 0, 3)).reshape(3, H, BUB)
    row_i = tile_ids // N_GY
    row_j = tile_ids % N_GY
    state_list = []
    hist_list = []
    for d, (dx, dy) in enumerate(neighbours):
        source = (row_i - dx) % N_GX * N_GY + (row_j - dy) % N_GY
        state_list.append(jnp.transpose(out_state[source, d], (1, 0, 2)).reshape(6, ARR))
        hist_list.append(jnp.transpose(out_hist[source, d], (1, 2, 0, 3)).reshape(3, H, ARR))
    return (new_speed, new_position, new_history, jnp.stack(state_list), jnp.stack(hist_list))
```

```python
import functools

import jax
import jax.numpy as jnp
from jax import lax
from jax.experimental import pallas as pl
from jax.experimental.pallas import tpu as pltpu
from jax.sharding import PartitionSpec as P

neighbours = ((-1, -1), (-1, 0), (-1, 1), (0, -1), (0, 1), (1, -1), (1, 0), (1, 1))
step_dt = 0.1
relax_tau = 0.5
basset_coef = 0.3
MESH = pl.DeviceIdType.MESH
F32 = jnp.float32
BF16 = jnp.bfloat16


def basis_rows(s):
    return (
        -s * (s - 1.0) * (s - 2.0) / 6.0,
        (s + 1.0) * (s - 1.0) * (s - 2.0) / 2.0,
        -(s + 1.0) * s * (s - 2.0) / 2.0,
        (s + 1.0) * s * (s - 1.0) / 6.0,
    )


def pick_weight(d, w):
    out = jnp.where(d == 0, w[0], 0.0)
    for p in range(1, 4):
        out = jnp.where(d == p, w[p], out)
    return out


def split(v):
    hi = v.astype(BF16)
    return hi, (v - hi.astype(F32)).astype(BF16)


def iota(shape, dim):
    return lax.broadcasted_iota(jnp.int32, shape, dim)


def contract_lanes(a, b):
    return lax.dot_general(a, b, (((1,), (1,)), ((), ())), preferred_element_type=F32)


def main_kernel(
    sizes,
    live, counts, slots, cell, shift, frac, speed, flow, hist,
    res, rec_hist, rec_state,
    f_buf, h_buf, a3, w3, sx, rx, sy, ry, b3, fl, sel, mslot, hhi, hlo, s_hist, s_state,
    sem_f, sem_h, sem_xs, sem_xr, sem_ys, sem_yr, sem_rs, sem_rr, sem_ss, sem_sr,
):
    nx, ny, nz, nb, cap, steps, gx_n, gy_n = sizes
    zx = nz * nx
    xh = 4 * nz
    half = 2 * nz
    k3 = 3 * zx
    chunk = 256
    gx = lax.axis_index("gx")
    gy = lax.axis_index("gy")
    wrap_x = lambda i: lax.rem(gx + i + gx_n, gx_n)
    wrap_y = lambda i: lax.rem(gy + i + gy_n, gy_n)

    f_copies = [pltpu.make_async_copy(flow.at[c], f_buf.at[c], sem_f.at[c]) for c in range(6)]
    h_copies = [pltpu.make_async_copy(hist.at[c], h_buf.at[c], sem_h.at[c]) for c in range(3)]
    for cp in f_copies + h_copies:
        cp.start()

    barrier = pltpu.get_barrier_semaphore()
    for dx, dy in neighbours:
        pl.semaphore_signal(barrier, inc=1, device_id=(wrap_x(dx), wrap_y(dy)), device_id_type=MESH)

    base = cell[...] + shift[...]
    s = frac[...] - shift[...].astype(F32)
    wxr = [w[0:1] for w in basis_rows(s)]
    wyr = [w[1:2] for w in basis_rows(s)]
    wzr = [w[2:3] for w in basis_rows(s)]
    bx, by, bz = base[0:1], base[1:2], base[2:3]

    def cut(v, j):
        return v[:, j * chunk : (j + 1) * chunk]

    def along_x(x, j):
        return pick_weight(x - cut(bx, j) + 1, [cut(w, j) for w in wxr])

    def along_y(y, j):
        return pick_weight(y - cut(by, j) + 1, [cut(w, j) for w in wyr])

    def along_z(z, j):
        return pick_weight((z - cut(bz, j) + 1 + nz) % nz, [cut(w, j) for w in wzr])

    for c in range(6):
        f_copies[c].wait()
        for z in range(nz):
            sx[0, c, 2 * z : 2 * z + 2, :] = f_buf[c, z, 0:2, :]
            sx[1, c, 2 * z : 2 * z + 2, :] = f_buf[c, z, nx - 2 : nx, :]
    pl.semaphore_wait(barrier, 8)
    x_copies = [
        pltpu.make_async_remote_copy(
            src_ref=sx.at[side], dst_ref=rx.at[1 - side], send_sem=sem_xs.at[side],
            recv_sem=sem_xr.at[1 - side], device_id=(wrap_x(2 * side - 1), gy), device_id_type=MESH,
        )
        for side in range(2)
    ]
    for cp in x_copies:
        cp.start()

    sy[...] = jnp.zeros_like(sy)
    for c in range(6):
        t = jnp.transpose(f_buf[c].reshape(zx, ny))
        hi, lo = split(t)
        rows = slice(c * ny, (c + 1) * ny)
        a3[rows, 0:zx] = hi
        a3[rows, zx : 2 * zx] = lo
        a3[rows, 2 * zx : 3 * zx] = hi
        sy[0, 2 * c : 2 * c + 2, 0:zx] = t[0:2]
        sy[1, 2 * c : 2 * c + 2, 0:zx] = t[ny - 2 : ny]

    def build_w(j):
        cols = slice(j * chunk, (j + 1) * chunk)
        wx = along_x(iota((nx, chunk), 0), j)
        wz = along_z(iota((nz, chunk), 0), j)
        for z in range(nz):
            hi, lo = split(wx * wz[z : z + 1])
            w3[z * nx : (z + 1) * nx, cols] = hi
            w3[zx + z * nx : zx + (z + 1) * nx, cols] = hi
            w3[2 * zx + z * nx : 2 * zx + (z + 1) * nx, cols] = lo
        r = iota((xh, chunk), 0)
        side = jnp.where(r < half, -2, nx)
        hi, lo = split(along_x(side + r % 2, j) * along_z((r % half) // 2, j))
        w3[k3 : k3 + xh, cols] = hi
        w3[k3 + xh : k3 + 2 * xh, cols] = hi
        w3[k3 + 2 * xh : k3 + 3 * xh, cols] = lo
        w3[k3 + 3 * xh : k3 + 4 * xh, cols] = jnp.zeros_like(lo)

    def local_part(j, lo_k, hi_k):
        cols = slice(j * chunk, (j + 1) * chunk)
        p = jnp.dot(a3[:, lo_k:hi_k], w3[lo_k:hi_k, cols], preferred_element_type=F32)
        wy = along_y(iota((ny, chunk), 0), j)
        return jnp.sum(p.reshape(6, ny, chunk) * wy[None], axis=1)

    fl[...] = jnp.zeros_like(fl)

    def add_local(j, lo_k, hi_k):
        cols = slice(j * chunk, (j + 1) * chunk)
        fl[0:6, cols] += local_part(j, lo_k, hi_k)

    chunks = nb // chunk
    build_w(0)
    add_local(0, 0, k3)

    for cp in x_copies:
        cp.wait()
    for c in range(6):
        block = jnp.concatenate([rx[0, c], rx[1, c], jnp.zeros((ny - xh, ny), F32)], axis=0)
        t = jnp.transpose(block)
        sy[0, 2 * c : 2 * c + 2, zx : zx + ny] = t[0:2]
        sy[1, 2 * c : 2 * c + 2, zx : zx + ny] = t[ny - 2 : ny]
        hi = t.astype(BF16).astype(F32)
        lo = t - hi
        rows = slice(c * ny, (c + 1) * ny)
        a3[rows, k3 : k3 + ny] = (hi + pltpu.roll(lo, xh, 1)).astype(BF16)
        a3[rows, k3 + ny : k3 + 2 * ny] = hi.astype(BF16)
    y_copies = [
        pltpu.make_async_remote_copy(
            src_ref=sy.at[side], dst_ref=ry.at[1 - side], send_sem=sem_ys.at[side],
            recv_sem=sem_yr.at[1 - side], device_id=(gx, wrap_y(2 * side - 1)), device_id_type=MESH,
        )
        for side in range(2)
    ]
    for cp in y_copies:
        cp.start()

    mslot[...] = jnp.zeros_like(mslot)
    mslot[0:8, 0:cap] = slots[0].astype(F32)
    cols_t = jnp.transpose(mslot[...])
    for d in range(8):
        col = cols_t[0:cap, d : d + 1]
        col = jnp.where(iota((cap, 1), 0) < counts[0, d], col, -1.0).astype(jnp.int32)
        sel[d * cap : (d + 1) * cap, :] = (iota((cap, nb), 1) == col).astype(F32).astype(BF16)
    karg = iota((steps, 128), 0).astype(F32) + 1.0
    quad = (jnp.sqrt(karg + 1.0) - jnp.sqrt(karg))[:, 0:1]
    tails = []
    for c in range(3):
        h_copies[c].wait()
        h = h_buf[c]
        tails.append(jnp.sum(h * quad, axis=0, keepdims=True))
        hi, lo = split(h)
        hhi[...] = hi
        hlo[...] = lo
        picked = contract_lanes(sel[...], hhi[...]) + contract_lanes(sel[...], hlo[...])
        picked = pltpu.roll(picked, 1, 1)
        for d in range(8):
            s_hist[d, :, c * steps : (c + 1) * steps] = picked[d * cap : (d + 1) * cap]
    tail = jnp.concatenate(tails, axis=0)
    r_copies = [
        pltpu.make_async_remote_copy(
            src_ref=s_hist.at[d], dst_ref=rec_hist.at[d], send_sem=sem_rs.at[d],
            recv_sem=sem_rr.at[d], device_id=(wrap_x(dx), wrap_y(dy)), device_id_type=MESH,
        )
        for d, (dx, dy) in enumerate(neighbours)
    ]
    for cp in r_copies:
        cp.start()

    for j in range(1, chunks):
        build_w(j)
        add_local(j, 0, k3 + 4 * xh)
    add_local(0, k3, k3 + 4 * xh)

    for cp in y_copies:
        cp.wait()
    for side in range(2):
        rows = slice(16 * side, 16 * side + 16)
        v = ry[side]
        hi, lo = split(v[:, 0:zx])
        b3[rows, 0:zx] = hi
        b3[rows, zx : 2 * zx] = lo
        b3[rows, 2 * zx : 3 * zx] = hi
        t = v[:, zx : zx + ny]
        thi = t.astype(BF16).astype(F32)
        b3[rows, k3 : k3 + ny] = (thi + pltpu.roll(t - thi, xh, 1)).astype(BF16)
        b3[rows, k3 + ny : k3 + 2 * ny] = thi.astype(BF16)
    pb = jnp.dot(b3[...], w3[...], preferred_element_type=F32)
    wyh = [pick_weight(y - by + 1, wyr) for y in (-2, -1, ny, ny + 1)]
    fluid = []
    for c in range(6):
        extra = pb[2 * c : 2 * c + 1] * wyh[0] + pb[2 * c + 1 : 2 * c + 2] * wyh[1]
        extra += pb[16 + 2 * c : 17 + 2 * c] * wyh[2] + pb[17 + 2 * c : 18 + 2 * c] * wyh[3]
        fluid.append(fl[c : c + 1, :] + extra)
    fluid_u = jnp.concatenate(fluid[0:3], axis=0)
    fluid_a = jnp.concatenate(fluid[3:6], axis=0)

    v0 = speed[...]

    def rate(v):
        return 3.0 * fluid_a + (fluid_u - v) / relax_tau + basset_coef * (fluid_u - v + tail)

    v1 = v0 + step_dt * rate(v0)
    v2 = 0.75 * v0 + 0.25 * (v1 + step_dt * rate(v1))
    vn = v0 / 3.0 + 2.0 / 3.0 * (v2 + step_dt * rate(v2))
    posn = frac[...] + step_dt * (v0 / 6.0 + v1 / 6.0 + 2.0 * v2 / 3.0)
    keep = iota((3, nb), 1) < live[0]
    res[0:3, :] = jnp.where(keep, vn, 0.0)
    res[3:6, :] = jnp.where(keep, posn, 0.0)
    res[6:9, :] = jnp.where(keep, fluid_u - vn, 0.0)
    res[9:16, :] = jnp.zeros((7, nb), F32)
    hi, lo = split(res[...])
    st = contract_lanes(sel[...], hi) + contract_lanes(sel[...], lo)
    for d in range(8):
        s_state[d, :, 0:16] = st[d * cap : (d + 1) * cap]
        s_state[d, :, 16:128] = jnp.zeros((cap, 112), F32)
    s_copies = [
        pltpu.make_async_remote_copy(
            src_ref=s_state.at[d], dst_ref=rec_state.at[d], send_sem=sem_ss.at[d],
            recv_sem=sem_sr.at[d], device_id=(wrap_x(dx), wrap_y(dy)), device_id_type=MESH,
        )
        for d, (dx, dy) in enumerate(neighbours)
    ]
    for cp in s_copies:
        cp.start()
    for cp in r_copies + s_copies:
        cp.wait()


def finish_kernel(cap, steps, live, res, rec_hist, rec_state, hist, vn, posn, out_hist, arr_state, arr_hist):
    c = pl.program_id(0)
    j = pl.program_id(1)
    wide = hist.shape[2]

    keep = (iota((1, wide), 1) + j * wide) < live[0]
    h = hist[0]
    top = res[pl.ds(6 + c, 1), pl.ds(pl.multiple_of(j * wide, wide), wide)]
    moved = jnp.where(iota(h.shape, 0) == 0, top, pltpu.roll(h, 1, 0))
    out_hist[0] = jnp.where(keep, moved, 0.0)

    @pl.when((c == 0) & (j == 0))
    def _():
        vn[...] = res[0:3, :]
        posn[...] = res[3:6, :]
        first = iota((cap, steps), 1) == 0
        for d in range(8):
            for cc in range(3):
                col = rec_state[d, :, 6 + cc : 7 + cc]
                arr_hist[d, cc] = jnp.where(first, col, rec_hist[d, :, cc * steps : (cc + 1) * steps])
        t = jnp.transpose(rec_state[...].reshape(8 * cap, 128))
        for d in range(8):
            arr_state[:, d, :] = t[0:6, d * cap : (d + 1) * cap]


def on_device(flow, cell, shift, frac, speed, hist, live, slots, counts):
    _, nz, nx, ny = flow.shape
    nb = speed.shape[1]
    steps = hist.shape[1]
    cap = slots.shape[2]
    zx = nz * nx
    k3 = 3 * zx + 4 * 4 * nz
    sizes = (nx, ny, nz, nb, cap, steps, lax.axis_size("gx"), lax.axis_size("gy"))
    vmem = pl.BlockSpec(memory_space=pltpu.VMEM)
    smem = pl.BlockSpec(memory_space=pltpu.SMEM)
    any_ = pl.BlockSpec(memory_space=pl.ANY)
    dma = pltpu.SemaphoreType.DMA
    res, rec_hist, rec_state = pl.pallas_call(
        functools.partial(main_kernel, sizes),
        out_shape=(
            jax.ShapeDtypeStruct((16, nb), F32),
            jax.ShapeDtypeStruct((8, cap, 3 * steps), F32),
            jax.ShapeDtypeStruct((8, cap, 128), F32),
        ),
        in_specs=[smem, smem, vmem, vmem, vmem, vmem, vmem, any_, any_],
        out_specs=[vmem, vmem, vmem],
        scratch_shapes=[
            pltpu.VMEM((6, nz, nx, ny), F32),
            pltpu.VMEM((3, steps, nb), F32),
            pltpu.VMEM((6 * ny, k3), BF16),
            pltpu.VMEM((k3, nb), BF16),
            pltpu.VMEM((2, 6, 2 * nz, ny), F32),
            pltpu.VMEM((2, 6, 2 * nz, ny), F32),
            pltpu.VMEM((2, 16, zx + ny), F32),
            pltpu.VMEM((2, 16, zx + ny), F32),
            pltpu.VMEM((32, k3), BF16),
            pltpu.VMEM((8, nb), F32),
            pltpu.VMEM((8 * cap, nb), BF16),
            pltpu.VMEM((128, 128), F32),
            pltpu.VMEM((steps, nb), BF16),
            pltpu.VMEM((steps, nb), BF16),
            pltpu.VMEM((8, cap, 3 * steps), F32),
            pltpu.VMEM((8, cap, 128), F32),
            dma((6,)), dma((3,)), dma((2,)), dma((2,)), dma((2,)), dma((2,)),
            dma((8,)), dma((8,)), dma((8,)), dma((8,)),
        ],
        compiler_params=pltpu.CompilerParams(
            collective_id=0, has_side_effects=True, vmem_limit_bytes=48 * 2**20
        ),
        name="interpolate_and_migrate",
    )(live, counts, slots, cell, shift, frac, speed, flow, hist)

    parts = 2
    whole = lambda *shape: pl.BlockSpec(shape, lambda c, j: (0,) * len(shape))
    vn, posn, out_hist, arr_state, arr_hist = pl.pallas_call(
        functools.partial(finish_kernel, cap, steps),
        grid=(3, parts),
        out_shape=(
            jax.ShapeDtypeStruct((3, nb), F32),
            jax.ShapeDtypeStruct((3, nb), F32),
            jax.ShapeDtypeStruct((3, steps, nb), F32),
            jax.ShapeDtypeStruct((6, 8, cap), F32),
            jax.ShapeDtypeStruct((8, 3, cap, steps), F32),
        ),
        in_specs=[
            smem,
            whole(16, nb),
            whole(8, cap, 3 * steps),
            whole(8, cap, 128),
            pl.BlockSpec((1, steps, nb // parts), lambda c, j: (c, 0, j)),
        ],
        out_specs=[
            whole(3, nb),
            whole(3, nb),
            pl.BlockSpec((1, steps, nb // parts), lambda c, j: (c, 0, j)),
            whole(6, 8, cap),
            whole(8, 3, cap, steps),
        ],
        compiler_params=pltpu.CompilerParams(vmem_limit_bytes=32 * 2**20),
        name="shift_history",
    )(live, res, rec_hist, rec_state, hist)
    return (
        vn,
        posn,
        out_hist,
        jnp.transpose(arr_state, (1, 0, 2)),
        jnp.transpose(arr_hist, (0, 1, 3, 2)),
    )


def solution(mesh):
    placed = (
        P(None, None, "gx", "gy"),
        P(None, ("gx", "gy")),
        P(None, ("gx", "gy")),
        P(None, ("gx", "gy")),
        P(None, ("gx", "gy")),
        P(None, None, ("gx", "gy")),
        P(("gx", "gy")),
        P(("gx", "gy"), None, None),
        P(("gx", "gy"), None),
    )
    return jax.shard_map(
        on_device,
        mesh=mesh,
        in_specs=placed,
        out_specs=(
            P(None, ("gx", "gy")),
            P(None, ("gx", "gy")),
            P(None, None, ("gx", "gy")),
            P(None, None, ("gx", "gy")),
            P(None, None, None, ("gx", "gy")),
        ),
        check_vma=False,
    )
```

```python
import functools

import jax
import jax.numpy as jnp
from jax import lax
from jax.experimental import pallas as pl
from jax.experimental.pallas import tpu as pltpu
from jax.sharding import PartitionSpec as P

neighbours = ((-1, -1), (-1, 0), (-1, 1), (0, -1), (0, 1), (1, -1), (1, 0), (1, 1))
step_dt = 0.1
relax_tau = 0.5
basset_coef = 0.3
MESH = pl.DeviceIdType.MESH
F32 = jnp.float32
BF16 = jnp.bfloat16


def basis_rows(s):
    return (
        -s * (s - 1.0) * (s - 2.0) / 6.0,
        (s + 1.0) * (s - 1.0) * (s - 2.0) / 2.0,
        -(s + 1.0) * s * (s - 2.0) / 2.0,
        (s + 1.0) * s * (s - 1.0) / 6.0,
    )


def pick_weight(d, w):
    out = jnp.where(d == 0, w[0], 0.0)
    for p in range(1, 4):
        out = jnp.where(d == p, w[p], out)
    return out


def split(v):
    hi = v.astype(BF16)
    return hi, (v - hi.astype(F32)).astype(BF16)


def iota(shape, dim):
    return lax.broadcasted_iota(jnp.int32, shape, dim)


def contract_lanes(a, b):
    return lax.dot_general(a, b, (((1,), (1,)), ((), ())), preferred_element_type=F32)


def main_kernel(
    sizes,
    live, counts, slots, cell, shift, frac, speed, flow, hist,
    res, rec_hist, rec_state, moved,
    i_cell, i_shift, i_frac, i_speed, i_slots, i_counts,
    f_buf, h_buf, a3, w3, sx, rx, ty, sy, ry, fl, sel, mslot, hhi, hlo, tail_s, s_hist, s_state,
    sem_i, sem_f, sem_h, sem_xs, sem_xr, sem_ys, sem_yr, sem_rs, sem_rr, sem_ss, sem_sr,
):
    nx, ny, nz, nb, cap, steps, gx_n, gy_n = sizes
    zx = nz * nx
    xh = 4 * nz
    half = 2 * nz
    k3 = 3 * zx
    chunk = 256
    m = 6 * ny
    gx = lax.axis_index("gx")
    gy = lax.axis_index("gy")
    wrap_x = lambda i: lax.rem(gx + i + gx_n, gx_n)
    wrap_y = lambda i: lax.rem(gy + i + gy_n, gy_n)

    def f_copy(c):
        return pltpu.make_async_copy(flow.at[c], f_buf.at[c], sem_f.at[c])

    def h_copy(c):
        return pltpu.make_async_copy(hist.at[c], h_buf.at[c], sem_h.at[c])

    small = [
        pltpu.make_async_copy(a, b, sem_i.at[i])
        for i, (a, b) in enumerate(
            (
                (cell, i_cell), (shift, i_shift), (frac, i_frac), (speed, i_speed),
                (slots, i_slots), (counts, i_counts),
            )
        )
    ]
    for c in range(6):
        f_copy(c).start()
    for cp in small:
        cp.start()
    for c in range(3):
        h_copy(c).start()

    barrier = pltpu.get_barrier_semaphore()
    for dx, dy in neighbours:
        pl.semaphore_signal(barrier, inc=1, device_id=(wrap_x(dx), wrap_y(dy)), device_id_type=MESH)
    sy[...] = jnp.zeros_like(sy)

    def pack_x(c, _):
        f_copy(c).wait()
        for z in range(nz):
            sx[0, c, 2 * z : 2 * z + 2, :] = f_buf[c, z, 0:2, :]
            sx[1, c, 2 * z : 2 * z + 2, :] = f_buf[c, z, nx - 2 : nx, :]
        return 0

    lax.fori_loop(0, 6, pack_x, 0)
    pl.semaphore_wait(barrier, 8)
    x_copies = [
        pltpu.make_async_remote_copy(
            src_ref=sx.at[side], dst_ref=rx.at[1 - side], send_sem=sem_xs.at[side],
            recv_sem=sem_xr.at[1 - side], device_id=(wrap_x(2 * side - 1), gy), device_id_type=MESH,
        )
        for side in range(2)
    ]
    for cp in x_copies:
        cp.start()

    for cp in small:
        cp.wait()

    def lanes_of(j):
        return pl.ds(pl.multiple_of(j * chunk, chunk), chunk)

    def build_w(j, _):
        cols = lanes_of(j)
        base = i_cell[:, cols] + i_shift[:, cols]
        w = basis_rows(i_frac[:, cols] - i_shift[:, cols].astype(F32))

        def along(pos, dim):
            d = pos - base[dim : dim + 1] + 1
            if dim == 2:
                d = jnp.where(d < 0, d + nz, jnp.where(d >= nz, d - nz, d))
            return pick_weight(d, [v[dim : dim + 1] for v in w])

        wx = along(iota((nx, chunk), 0), 0)
        wz = along(iota((nz, chunk), 0), 2)
        for z in range(nz):
            hi, lo = split(wx * wz[z : z + 1])
            w3[z * nx : (z + 1) * nx, cols] = hi
            w3[zx + z * nx : zx + (z + 1) * nx, cols] = hi
            w3[2 * zx + z * nx : 2 * zx + (z + 1) * nx, cols] = lo
        r = iota((xh, chunk), 0)
        far = r >= half
        q = jnp.where(far, r - half, r)
        hi, lo = split(along(jnp.where(far, nx, -2) + (q & 1), 0) * along(q >> 1, 2))
        w3[k3 : k3 + xh, cols] = hi
        w3[k3 + xh : k3 + 2 * xh, cols] = hi
        w3[k3 + 2 * xh : k3 + 3 * xh, cols] = lo
        w3[k3 + 3 * xh : k3 + 4 * xh, cols] = jnp.zeros_like(lo)
        return 0

    lax.fori_loop(0, nb // chunk, build_w, 0)

    def rows_of(c):
        return pl.ds(pl.multiple_of(c * ny, ny), ny)

    def turn(c, _):
        t = jnp.transpose(f_buf[c].reshape(zx, ny))
        hi, lo = split(t)
        rows = rows_of(c)
        a3[rows, 0:zx] = hi
        a3[rows, zx : 2 * zx] = lo
        a3[rows, 2 * zx : 3 * zx] = hi
        ty[c, 0:2, 0:zx] = t[0:2]
        ty[c, 2:4, 0:zx] = t[ny - 2 : ny]
        return 0

    lax.fori_loop(0, 6, turn, 0)

    for cp in x_copies:
        cp.wait()

    def turn_x(c, _):
        block = jnp.concatenate([rx[0, c], rx[1, c], jnp.zeros((ny - xh, ny), F32)], axis=0)
        t = jnp.transpose(block)
        ty[c, 0:2, zx : zx + ny] = t[0:2]
        ty[c, 2:4, zx : zx + ny] = t[ny - 2 : ny]
        hi = t.astype(BF16).astype(F32)
        lo = t - hi
        rows = rows_of(c)
        a3[rows, k3 : k3 + ny] = (hi + pltpu.roll(lo, xh, 1)).astype(BF16)
        a3[rows, k3 + ny : k3 + 2 * ny] = hi.astype(BF16)
        return 0

    lax.fori_loop(0, 6, turn_x, 0)
    for c in range(6):
        sy[0, 2 * c : 2 * c + 2, :] = ty[c, 0:2, :]
        sy[1, 2 * c : 2 * c + 2, :] = ty[c, 2:4, :]
    y_copies = [
        pltpu.make_async_remote_copy(
            src_ref=sy.at[side], dst_ref=ry.at[1 - side], send_sem=sem_ys.at[side],
            recv_sem=sem_yr.at[1 - side], device_id=(gx, wrap_y(2 * side - 1)), device_id_type=MESH,
        )
        for side in range(2)
    ]
    for cp in y_copies:
        cp.start()

    mslot[...] = jnp.zeros_like(mslot)
    mslot[0:8, 0:cap] = i_slots[0].astype(F32)
    cols_t = jnp.transpose(mslot[...])
    for d in range(8):
        col = cols_t[0:cap, d : d + 1]
        col = jnp.where(iota((cap, 1), 0) < i_counts[0, d], col, -1.0).astype(jnp.int32)
        sel[d * cap : (d + 1) * cap, :] = (iota((cap, nb), 1) == col).astype(F32).astype(BF16)
    karg = iota((steps, 128), 0).astype(F32) + 1.0
    quad = (jnp.sqrt(karg + 1.0) - jnp.sqrt(karg))[:, 0:1]

    def pick_history(c, _):
        h_copy(c).wait()
        h = h_buf[c]
        tail_s[c] = jnp.sum(h * quad, axis=0, keepdims=True)
        hi, lo = split(h)
        hhi[...] = hi
        hlo[...] = lo
        picked = contract_lanes(sel[...], hhi[...]) + contract_lanes(sel[...], hlo[...])
        picked = pltpu.roll(picked, 1, 1)
        s_hist[:, :, pl.ds(pl.multiple_of(c * steps, steps), steps)] = picked.reshape(8, cap, steps)
        return 0

    lax.fori_loop(0, 3, pick_history, 0)
    r_copies = [
        pltpu.make_async_remote_copy(
            src_ref=s_hist.at[d], dst_ref=rec_hist.at[d], send_sem=sem_rs.at[d],
            recv_sem=sem_rr.at[d], device_id=(wrap_x(dx), wrap_y(dy)), device_id_type=MESH,
        )
        for d, (dx, dy) in enumerate(neighbours)
    ]
    for cp in r_copies:
        cp.start()

    for cp in y_copies:
        cp.wait()
    for side in range(2):
        rows = slice(m + 16 * side, m + 16 * side + 16)
        v = ry[side]
        hi, lo = split(v[:, 0:zx])
        a3[rows, 0:zx] = hi
        a3[rows, zx : 2 * zx] = lo
        a3[rows, 2 * zx : 3 * zx] = hi
        t = v[:, zx : zx + ny]
        thi = t.astype(BF16).astype(F32)
        a3[rows, k3 : k3 + ny] = (thi + pltpu.roll(t - thi, xh, 1)).astype(BF16)
        a3[rows, k3 + ny : k3 + 2 * ny] = thi.astype(BF16)

    def interpolate(j, _):
        cols = lanes_of(j)
        p = jnp.dot(a3[...], w3[:, cols], preferred_element_type=F32)
        shift_y = i_shift[1:2, cols]
        by = i_cell[1:2, cols] + shift_y
        w = basis_rows(i_frac[1:2, cols] - shift_y.astype(F32))
        wy = pick_weight(iota((ny, chunk), 0) - by + 1, w)
        fl[0:6, cols] = jnp.sum(p[0:m].reshape(6, ny, chunk) * wy[None], axis=1)
        wyh = [pick_weight(y - by + 1, w) for y in (-2, -1, ny, ny + 1)]
        for c in range(6):
            at = m + 2 * c
            extra = p[at : at + 1] * wyh[0] + p[at + 1 : at + 2] * wyh[1]
            at += 16
            extra += p[at : at + 1] * wyh[2] + p[at + 1 : at + 2] * wyh[3]
            fl[c : c + 1, cols] += extra
        return 0

    lax.fori_loop(0, nb // chunk, interpolate, 0)

    fluid_u = fl[0:3, :]
    fluid_a = fl[3:6, :]
    v0 = i_speed[...]
    tail = jnp.concatenate([tail_s[c] for c in range(3)], axis=0)

    def rate(v):
        return 3.0 * fluid_a + (fluid_u - v) / relax_tau + basset_coef * (fluid_u - v + tail)

    v1 = v0 + step_dt * rate(v0)
    v2 = 0.75 * v0 + 0.25 * (v1 + step_dt * rate(v1))
    vn = v0 / 3.0 + 2.0 / 3.0 * (v2 + step_dt * rate(v2))
    posn = i_frac[...] + step_dt * (v0 / 6.0 + v1 / 6.0 + 2.0 * v2 / 3.0)
    keep = iota((3, nb), 1) < live[0]
    res[0:3, :] = jnp.where(keep, vn, 0.0)
    res[3:6, :] = jnp.where(keep, posn, 0.0)
    res[6:9, :] = jnp.where(keep, fluid_u - vn, 0.0)
    res[9:16, :] = jnp.zeros((7, nb), F32)
    hi, lo = split(res[...])
    st = contract_lanes(sel[...], hi) + contract_lanes(sel[...], lo)
    s_state[...] = jnp.zeros_like(s_state)
    s_state[:, :, 0:16] = st.reshape(8, cap, 16)
    s_copies = [
        pltpu.make_async_remote_copy(
            src_ref=s_state.at[d], dst_ref=rec_state.at[d], send_sem=sem_ss.at[d],
            recv_sem=sem_sr.at[d], device_id=(wrap_x(dx), wrap_y(dy)), device_id_type=MESH,
        )
        for d, (dx, dy) in enumerate(neighbours)
    ]
    for cp in s_copies:
        cp.start()

    for c in range(3):
        fl[c : c + 1, :] = res[6 + c : 7 + c, :]

    def move(i, _):
        cols = pl.ds(pl.multiple_of(i * 128, 128), 128)
        alive = (iota((1, 128), 1) + i * 128) < live[0]
        top = fl[:, cols]
        for c in range(3):
            h = pltpu.roll(h_buf[c, :, cols], 1, 0)
            h = jnp.where(iota((steps, 128), 0) == 0, top[c : c + 1], h)
            moved[c, :, cols] = jnp.where(alive, h, 0.0)
        return 0

    lax.fori_loop(0, nb // 128, move, 0)
    for cp in r_copies + s_copies:
        cp.wait()


def finish_kernel(
    cap, steps,
    res, rec_hist, rec_state, moved,
    vn, posn, out_hist, arr_state, arr_hist,
    b_vn, b_posn, b_state, b_hist, sems,
):
    copies = [pltpu.make_async_copy(moved, out_hist, sems.at[0])]
    copies[0].start()

    def send(src, dst):
        cp = pltpu.make_async_copy(src, dst, sems.at[len(copies)])
        cp.start()
        copies.append(cp)

    b_vn[...] = res[0:3, :]
    send(b_vn, vn)
    b_posn[...] = res[3:6, :]
    send(b_posn, posn)
    t = jnp.transpose(rec_state[...].reshape(8 * cap, 128))
    for d in range(8):
        b_state[:, d, :] = t[0:6, d * cap : (d + 1) * cap]
    send(b_state, arr_state)
    first = iota((cap, steps), 1) == 0
    for d in range(8):
        for c in range(3):
            col = rec_state[d, :, 6 + c : 7 + c]
            b_hist[d, c] = jnp.where(first, col, rec_hist[d, :, c * steps : (c + 1) * steps])
    send(b_hist, arr_hist)
    for cp in copies:
        cp.wait()


def on_device(flow, cell, shift, frac, speed, hist, live, slots, counts):
    _, nz, nx, ny = flow.shape
    nb = speed.shape[1]
    steps = hist.shape[1]
    cap = slots.shape[2]
    zx = nz * nx
    k3 = 3 * zx + 4 * 4 * nz
    sizes = (nx, ny, nz, nb, cap, steps, lax.axis_size("gx"), lax.axis_size("gy"))
    vmem = pl.BlockSpec(memory_space=pltpu.VMEM)
    hbm = pl.BlockSpec(memory_space=pltpu.HBM)
    dma = pltpu.SemaphoreType.DMA
    I32 = jnp.int32
    inputs = (counts, slots, cell, shift, frac, speed, flow, hist)
    gathered = pl.pallas_call(
        functools.partial(main_kernel, sizes),
        out_shape=(
            jax.ShapeDtypeStruct((16, nb), F32),
            jax.ShapeDtypeStruct((8, cap, 3 * steps), F32),
            jax.ShapeDtypeStruct((8, cap, 128), F32),
            jax.ShapeDtypeStruct((3, steps, nb), F32),
        ),
        in_specs=[pl.BlockSpec(memory_space=pltpu.SMEM)] + [hbm] * 8,
        out_specs=[vmem] * 4,
        scratch_shapes=[
            pltpu.VMEM((3, nb), I32),
            pltpu.VMEM((3, nb), I32),
            pltpu.VMEM((3, nb), F32),
            pltpu.VMEM((3, nb), F32),
            pltpu.VMEM((1, 8, cap), I32),
            pltpu.SMEM((1, 8), I32),
            pltpu.VMEM((6, nz, nx, ny), F32),
            pltpu.VMEM((3, steps, nb), F32),
            pltpu.VMEM((6 * ny + 32, k3), BF16),
            pltpu.VMEM((k3, nb), BF16),
            pltpu.VMEM((2, 6, 2 * nz, ny), F32),
            pltpu.VMEM((2, 6, 2 * nz, ny), F32),
            pltpu.VMEM((6, 8, zx + ny), F32),
            pltpu.VMEM((2, 16, zx + ny), F32),
            pltpu.VMEM((2, 16, zx + ny), F32),
            pltpu.VMEM((8, nb), F32),
            pltpu.VMEM((8 * cap, nb), BF16),
            pltpu.VMEM((128, 128), F32),
            pltpu.VMEM((steps, nb), BF16),
            pltpu.VMEM((steps, nb), BF16),
            pltpu.VMEM((3, 1, nb), F32),
            pltpu.VMEM((8, cap, 3 * steps), F32),
            pltpu.VMEM((8, cap, 128), F32),
            dma((6,)), dma((6,)), dma((3,)), dma((2,)), dma((2,)), dma((2,)), dma((2,)),
            dma((8,)), dma((8,)), dma((8,)), dma((8,)),
        ],
        compiler_params=pltpu.CompilerParams(
            collective_id=0, has_side_effects=True, vmem_limit_bytes=44 * 2**20
        ),
        name="interpolate_and_migrate",
    )(live, *(pltpu.with_memory_space_constraint(v, pltpu.HBM) for v in inputs))

    vn, posn, out_hist, arr_state, arr_hist = pl.pallas_call(
        functools.partial(finish_kernel, cap, steps),
        out_shape=(
            jax.ShapeDtypeStruct((3, nb), F32),
            jax.ShapeDtypeStruct((3, nb), F32),
            jax.ShapeDtypeStruct((3, steps, nb), F32),
            jax.ShapeDtypeStruct((6, 8, cap), F32),
            jax.ShapeDtypeStruct((8, 3, cap, steps), F32),
        ),
        in_specs=[vmem] * 4,
        out_specs=[hbm] * 5,
        scratch_shapes=[
            pltpu.VMEM((3, nb), F32),
            pltpu.VMEM((3, nb), F32),
            pltpu.VMEM((6, 8, cap), F32),
            pltpu.VMEM((8, 3, cap, steps), F32),
            dma((5,)),
        ],
        compiler_params=pltpu.CompilerParams(vmem_limit_bytes=32 * 2**20),
        name="write_results",
    )(*gathered)
    return (
        vn,
        posn,
        out_hist,
        jnp.transpose(arr_state, (1, 0, 2)),
        jnp.transpose(arr_hist, (0, 1, 3, 2)),
    )


def solution(mesh):
    placed = (
        P(None, None, "gx", "gy"),
        P(None, ("gx", "gy")),
        P(None, ("gx", "gy")),
        P(None, ("gx", "gy")),
        P(None, ("gx", "gy")),
        P(None, None, ("gx", "gy")),
        P(("gx", "gy")),
        P(("gx", "gy"), None, None),
        P(("gx", "gy"), None),
    )
    return jax.shard_map(
        on_device,
        mesh=mesh,
        in_specs=placed,
        out_specs=(
            P(None, ("gx", "gy")),
            P(None, ("gx", "gy")),
            P(None, None, ("gx", "gy")),
            P(None, None, ("gx", "gy")),
            P(None, None, None, ("gx", "gy")),
        ),
        check_vma=False,
    )
```

```python
import functools

import jax
import jax.numpy as jnp
from jax import lax
from jax.experimental import pallas as pl
from jax.experimental.pallas import tpu as pltpu
from jax.sharding import PartitionSpec as P

neighbours = ((-1, -1), (-1, 0), (-1, 1), (0, -1), (0, 1), (1, -1), (1, 0), (1, 1))
step_dt = 0.1
relax_tau = 0.5
basset_coef = 0.3
MESH = pl.DeviceIdType.MESH
F32 = jnp.float32
BF16 = jnp.bfloat16


def basis_rows(s):
    return (
        -s * (s - 1.0) * (s - 2.0) / 6.0,
        (s + 1.0) * (s - 1.0) * (s - 2.0) / 2.0,
        -(s + 1.0) * s * (s - 2.0) / 2.0,
        (s + 1.0) * s * (s - 1.0) / 6.0,
    )


def pick_weight(d, w):
    out = jnp.where(d == 0, w[0], 0.0)
    for p in range(1, 4):
        out = jnp.where(d == p, w[p], out)
    return out


def split(v):
    hi = v.astype(BF16)
    return hi, (v - hi.astype(F32)).astype(BF16)


def iota(shape, dim):
    return lax.broadcasted_iota(jnp.int32, shape, dim)


def contract_lanes(a, b):
    return lax.dot_general(a, b, (((1,), (1,)), ((), ())), preferred_element_type=F32)


def main_kernel(
    sizes,
    live, counts, slots, cell, shift, frac, speed, flow, hist,
    res, rec_hist, rec_state, moved,
    i_cell, i_shift, i_frac, i_speed, i_slots, i_counts,
    f_buf, h_buf, a3, w3, sx, rx, ty, sy, ry, fl, sel, mslot, hhi, hlo, tail_s, s_hist, s_state,
    sem_i, sem_f, sem_h, sem_xs, sem_xr, sem_ys, sem_yr, sem_rs, sem_rr, sem_ss, sem_sr,
):
    nx, ny, nz, nb, cap, steps, gx_n, gy_n = sizes
    zx = nz * nx
    xh = 4 * nz
    half = 2 * nz
    k3 = 3 * zx
    chunk = 512
    m = 6 * ny
    gx = lax.axis_index("gx")
    gy = lax.axis_index("gy")
    wrap_x = lambda i: lax.rem(gx + i + gx_n, gx_n)
    wrap_y = lambda i: lax.rem(gy + i + gy_n, gy_n)

    def f_copy(c):
        return pltpu.make_async_copy(flow.at[c], f_buf.at[c], sem_f.at[c])

    def h_copy(c):
        return pltpu.make_async_copy(hist.at[c], h_buf.at[c], sem_h.at[c])

    small = [
        pltpu.make_async_copy(a, b, sem_i.at[i])
        for i, (a, b) in enumerate(
            (
                (cell, i_cell), (shift, i_shift), (frac, i_frac), (speed, i_speed),
                (slots, i_slots), (counts, i_counts),
            )
        )
    ]
    for c in range(6):
        f_copy(c).start()
    for cp in small:
        cp.start()
    for c in range(3):
        h_copy(c).start()

    barrier = pltpu.get_barrier_semaphore()
    for dx, dy in neighbours:
        pl.semaphore_signal(barrier, inc=1, device_id=(wrap_x(dx), wrap_y(dy)), device_id_type=MESH)
    sy[...] = jnp.zeros_like(sy)

    def pack_x(c, _):
        f_copy(c).wait()
        for z in range(nz):
            sx[0, c, 2 * z : 2 * z + 2, :] = f_buf[c, z, 0:2, :]
            sx[1, c, 2 * z : 2 * z + 2, :] = f_buf[c, z, nx - 2 : nx, :]
        return 0

    lax.fori_loop(0, 6, pack_x, 0)
    pl.semaphore_wait(barrier, 8)
    x_copies = [
        pltpu.make_async_remote_copy(
            src_ref=sx.at[side], dst_ref=rx.at[1 - side], send_sem=sem_xs.at[side],
            recv_sem=sem_xr.at[1 - side], device_id=(wrap_x(2 * side - 1), gy), device_id_type=MESH,
        )
        for side in range(2)
    ]
    for cp in x_copies:
        cp.start()

    def lanes_of(j):
        return pl.ds(pl.multiple_of(j * chunk, chunk), chunk)

    def build_w(j, _):
        cols = lanes_of(j)
        base = i_cell[:, cols] + i_shift[:, cols]
        w = basis_rows(i_frac[:, cols] - i_shift[:, cols].astype(F32))

        def along(pos, dim):
            d = pos - base[dim : dim + 1] + 1
            if dim == 2:
                d = jnp.where(d < 0, d + nz, jnp.where(d >= nz, d - nz, d))
            return pick_weight(d, [v[dim : dim + 1] for v in w])

        wx = along(iota((nx, chunk), 0), 0)
        wz = along(iota((nz, chunk), 0), 2)
        for z in range(nz):
            hi, lo = split(wx * wz[z : z + 1])
            w3[z * nx : (z + 1) * nx, cols] = hi
            w3[zx + z * nx : zx + (z + 1) * nx, cols] = hi
            w3[2 * zx + z * nx : 2 * zx + (z + 1) * nx, cols] = lo
        r = iota((xh, chunk), 0)
        far = r >= half
        q = jnp.where(far, r - half, r)
        hi, lo = split(along(jnp.where(far, nx, -2) + (q & 1), 0) * along(q >> 1, 2))
        w3[k3 : k3 + xh, cols] = hi
        w3[k3 + xh : k3 + 2 * xh, cols] = hi
        w3[k3 + 2 * xh : k3 + 3 * xh, cols] = lo
        w3[k3 + 3 * xh : k3 + 4 * xh, cols] = jnp.zeros_like(lo)
        return 0

    def rows_of(c):
        return pl.ds(pl.multiple_of(c * ny, ny), ny)

    def turn(c, _):
        t = jnp.transpose(f_buf[c].reshape(zx, ny))
        hi, lo = split(t)
        rows = rows_of(c)
        a3[rows, 0:zx] = hi
        a3[rows, zx : 2 * zx] = lo
        a3[rows, 2 * zx : 3 * zx] = hi
        ty[c, 0:2, 0:zx] = t[0:2]
        ty[c, 2:4, 0:zx] = t[ny - 2 : ny]
        return 0

    lax.fori_loop(0, 6, turn, 0)

    for cp in x_copies:
        cp.wait()

    def turn_x(c, _):
        block = jnp.concatenate([rx[0, c], rx[1, c], jnp.zeros((ny - xh, ny), F32)], axis=0)
        t = jnp.transpose(block)
        ty[c, 0:2, zx : zx + ny] = t[0:2]
        ty[c, 2:4, zx : zx + ny] = t[ny - 2 : ny]
        hi = t.astype(BF16).astype(F32)
        lo = t - hi
        rows = rows_of(c)
        a3[rows, k3 : k3 + ny] = (hi + pltpu.roll(lo, xh, 1)).astype(BF16)
        a3[rows, k3 + ny : k3 + 2 * ny] = hi.astype(BF16)
        return 0

    lax.fori_loop(0, 6, turn_x, 0)
    for c in range(6):
        sy[0, 2 * c : 2 * c + 2, :] = ty[c, 0:2, :]
        sy[1, 2 * c : 2 * c + 2, :] = ty[c, 2:4, :]
    y_copies = [
        pltpu.make_async_remote_copy(
            src_ref=sy.at[side], dst_ref=ry.at[1 - side], send_sem=sem_ys.at[side],
            recv_sem=sem_yr.at[1 - side], device_id=(gx, wrap_y(2 * side - 1)), device_id_type=MESH,
        )
        for side in range(2)
    ]
    for cp in y_copies:
        cp.start()

    for cp in small:
        cp.wait()
    lax.fori_loop(0, nb // chunk, build_w, 0)

    mslot[...] = jnp.zeros_like(mslot)
    mslot[0:8, 0:cap] = i_slots[0].astype(F32)
    cols_t = jnp.transpose(mslot[...])
    for d in range(8):
        col = cols_t[0:cap, d : d + 1]
        col = jnp.where(iota((cap, 1), 0) < i_counts[0, d], col, -1.0).astype(jnp.int32)
        sel[d * cap : (d + 1) * cap, :] = (iota((cap, nb), 1) == col).astype(F32).astype(BF16)
    karg = iota((steps, 128), 0).astype(F32) + 1.0
    quad = (jnp.sqrt(karg + 1.0) - jnp.sqrt(karg))[:, 0:1]

    def pick_history(c, _):
        h_copy(c).wait()
        h = h_buf[c]
        tail_s[c] = jnp.sum(h * quad, axis=0, keepdims=True)
        hi, lo = split(h)
        hhi[...] = hi
        hlo[...] = lo
        picked = contract_lanes(sel[...], hhi[...]) + contract_lanes(sel[...], hlo[...])
        picked = pltpu.roll(picked, 1, 1)
        s_hist[:, :, pl.ds(pl.multiple_of(c * steps, steps), steps)] = picked.reshape(8, cap, steps)
        return 0

    lax.fori_loop(0, 3, pick_history, 0)
    r_copies = [
        pltpu.make_async_remote_copy(
            src_ref=s_hist.at[d], dst_ref=rec_hist.at[d], send_sem=sem_rs.at[d],
            recv_sem=sem_rr.at[d], device_id=(wrap_x(dx), wrap_y(dy)), device_id_type=MESH,
        )
        for d, (dx, dy) in enumerate(neighbours)
    ]
    for cp in r_copies:
        cp.start()

    for cp in y_copies:
        cp.wait()
    for side in range(2):
        rows = slice(m + 16 * side, m + 16 * side + 16)
        v = ry[side]
        hi, lo = split(v[:, 0:zx])
        a3[rows, 0:zx] = hi
        a3[rows, zx : 2 * zx] = lo
        a3[rows, 2 * zx : 3 * zx] = hi
        t = v[:, zx : zx + ny]
        thi = t.astype(BF16).astype(F32)
        a3[rows, k3 : k3 + ny] = (thi + pltpu.roll(t - thi, xh, 1)).astype(BF16)
        a3[rows, k3 + ny : k3 + 2 * ny] = thi.astype(BF16)

    def interpolate(j, _):
        cols = lanes_of(j)
        p = jnp.dot(a3[...], w3[:, cols], preferred_element_type=F32)
        shift_y = i_shift[1:2, cols]
        by = i_cell[1:2, cols] + shift_y
        w = basis_rows(i_frac[1:2, cols] - shift_y.astype(F32))
        wy = pick_weight(iota((ny, chunk), 0) - by + 1, w)
        fl[0:6, cols] = jnp.sum(p[0:m].reshape(6, ny, chunk) * wy[None], axis=1)
        wyh = [pick_weight(y - by + 1, w) for y in (-2, -1, ny, ny + 1)]
        for c in range(6):
            at = m + 2 * c
            extra = p[at : at + 1] * wyh[0] + p[at + 1 : at + 2] * wyh[1]
            at += 16
            extra += p[at : at + 1] * wyh[2] + p[at + 1 : at + 2] * wyh[3]
            fl[c : c + 1, cols] += extra
        return 0

    lax.fori_loop(0, nb // chunk, interpolate, 0)

    fluid_u = fl[0:3, :]
    fluid_a = fl[3:6, :]
    v0 = i_speed[...]
    tail = jnp.concatenate([tail_s[c] for c in range(3)], axis=0)

    def rate(v):
        return 3.0 * fluid_a + (fluid_u - v) / relax_tau + basset_coef * (fluid_u - v + tail)

    v1 = v0 + step_dt * rate(v0)
    v2 = 0.75 * v0 + 0.25 * (v1 + step_dt * rate(v1))
    vn = v0 / 3.0 + 2.0 / 3.0 * (v2 + step_dt * rate(v2))
    posn = i_frac[...] + step_dt * (v0 / 6.0 + v1 / 6.0 + 2.0 * v2 / 3.0)
    keep = iota((3, nb), 1) < live[0]
    res[0:3, :] = jnp.where(keep, vn, 0.0)
    res[3:6, :] = jnp.where(keep, posn, 0.0)
    res[6:9, :] = jnp.where(keep, fluid_u - vn, 0.0)
    res[9:16, :] = jnp.zeros((7, nb), F32)
    hi, lo = split(res[...])
    st = contract_lanes(sel[...], hi) + contract_lanes(sel[...], lo)
    s_state[...] = jnp.zeros_like(s_state)
    s_state[:, :, 0:16] = st.reshape(8, cap, 16)
    s_copies = [
        pltpu.make_async_remote_copy(
            src_ref=s_state.at[d], dst_ref=rec_state.at[d], send_sem=sem_ss.at[d],
            recv_sem=sem_sr.at[d], device_id=(wrap_x(dx), wrap_y(dy)), device_id_type=MESH,
        )
        for d, (dx, dy) in enumerate(neighbours)
    ]
    for cp in s_copies:
        cp.start()

    for c in range(3):
        fl[c : c + 1, :] = res[6 + c : 7 + c, :]

    def move(i, _):
        cols = pl.ds(pl.multiple_of(i * 128, 128), 128)
        alive = (iota((1, 128), 1) + i * 128) < live[0]
        top = fl[:, cols]
        for c in range(3):
            h = pltpu.roll(h_buf[c, :, cols], 1, 0)
            h = jnp.where(iota((steps, 128), 0) == 0, top[c : c + 1], h)
            moved[c, :, cols] = jnp.where(alive, h, 0.0)
        return 0

    lax.fori_loop(0, nb // 128, move, 0)
    for cp in r_copies + s_copies:
        cp.wait()


def finish_kernel(
    cap, steps,
    res, rec_hist, rec_state, moved,
    vn, posn, out_hist, arr_state, arr_hist,
    b_vn, b_posn, b_state, b_hist, sems,
):
    copies = [pltpu.make_async_copy(moved, out_hist, sems.at[0])]
    copies[0].start()

    def send(src, dst):
        cp = pltpu.make_async_copy(src, dst, sems.at[len(copies)])
        cp.start()
        copies.append(cp)

    b_vn[...] = res[0:3, :]
    send(b_vn, vn)
    b_posn[...] = res[3:6, :]
    send(b_posn, posn)
    t = jnp.transpose(rec_state[...].reshape(8 * cap, 128))
    for d in range(8):
        b_state[:, d, :] = t[0:6, d * cap : (d + 1) * cap]
    send(b_state, arr_state)
    first = iota((cap, steps), 1) == 0
    for d in range(8):
        for c in range(3):
            col = rec_state[d, :, 6 + c : 7 + c]
            b_hist[d, c] = jnp.where(first, col, rec_hist[d, :, c * steps : (c + 1) * steps])
    send(b_hist, arr_hist)
    for cp in copies:
        cp.wait()


def on_device(flow, cell, shift, frac, speed, hist, live, slots, counts):
    _, nz, nx, ny = flow.shape
    nb = speed.shape[1]
    steps = hist.shape[1]
    cap = slots.shape[2]
    zx = nz * nx
    k3 = 3 * zx + 4 * 4 * nz
    sizes = (nx, ny, nz, nb, cap, steps, lax.axis_size("gx"), lax.axis_size("gy"))
    vmem = pl.BlockSpec(memory_space=pltpu.VMEM)
    hbm = pl.BlockSpec(memory_space=pltpu.HBM)
    dma = pltpu.SemaphoreType.DMA
    I32 = jnp.int32
    inputs = (counts, slots, cell, shift, frac, speed, flow, hist)
    gathered = pl.pallas_call(
        functools.partial(main_kernel, sizes),
        out_shape=(
            jax.ShapeDtypeStruct((16, nb), F32),
            jax.ShapeDtypeStruct((8, cap, 3 * steps), F32),
            jax.ShapeDtypeStruct((8, cap, 128), F32),
            jax.ShapeDtypeStruct((3, steps, nb), F32),
        ),
        in_specs=[pl.BlockSpec(memory_space=pltpu.SMEM)] + [hbm] * 8,
        out_specs=[vmem] * 4,
        scratch_shapes=[
            pltpu.VMEM((3, nb), I32),
            pltpu.VMEM((3, nb), I32),
            pltpu.VMEM((3, nb), F32),
            pltpu.VMEM((3, nb), F32),
            pltpu.VMEM((1, 8, cap), I32),
            pltpu.SMEM((1, 8), I32),
            pltpu.VMEM((6, nz, nx, ny), F32),
            pltpu.VMEM((3, steps, nb), F32),
            pltpu.VMEM((6 * ny + 32, k3), BF16),
            pltpu.VMEM((k3, nb), BF16),
            pltpu.VMEM((2, 6, 2 * nz, ny), F32),
            pltpu.VMEM((2, 6, 2 * nz, ny), F32),
            pltpu.VMEM((6, 8, zx + ny), F32),
            pltpu.VMEM((2, 16, zx + ny), F32),
            pltpu.VMEM((2, 16, zx + ny), F32),
            pltpu.VMEM((8, nb), F32),
            pltpu.VMEM((8 * cap, nb), BF16),
            pltpu.VMEM((128, 128), F32),
            pltpu.VMEM((steps, nb), BF16),
            pltpu.VMEM((steps, nb), BF16),
            pltpu.VMEM((3, 1, nb), F32),
            pltpu.VMEM((8, cap, 3 * steps), F32),
            pltpu.VMEM((8, cap, 128), F32),
            dma((6,)), dma((6,)), dma((3,)), dma((2,)), dma((2,)), dma((2,)), dma((2,)),
            dma((8,)), dma((8,)), dma((8,)), dma((8,)),
        ],
        compiler_params=pltpu.CompilerParams(
            collective_id=0, has_side_effects=True, vmem_limit_bytes=44 * 2**20
        ),
        name="interpolate_and_migrate",
    )(live, *(pltpu.with_memory_space_constraint(v, pltpu.HBM) for v in inputs))

    vn, posn, out_hist, arr_state, arr_hist = pl.pallas_call(
        functools.partial(finish_kernel, cap, steps),
        out_shape=(
            jax.ShapeDtypeStruct((3, nb), F32),
            jax.ShapeDtypeStruct((3, nb), F32),
            jax.ShapeDtypeStruct((3, steps, nb), F32),
            jax.ShapeDtypeStruct((6, 8, cap), F32),
            jax.ShapeDtypeStruct((8, 3, cap, steps), F32),
        ),
        in_specs=[vmem] * 4,
        out_specs=[hbm] * 5,
        scratch_shapes=[
            pltpu.VMEM((3, nb), F32),
            pltpu.VMEM((3, nb), F32),
            pltpu.VMEM((6, 8, cap), F32),
            pltpu.VMEM((8, 3, cap, steps), F32),
            dma((5,)),
        ],
        compiler_params=pltpu.CompilerParams(vmem_limit_bytes=32 * 2**20),
        name="write_results",
    )(*gathered)
    return (
        vn,
        posn,
        out_hist,
        jnp.transpose(arr_state, (1, 0, 2)),
        jnp.transpose(arr_hist, (0, 1, 3, 2)),
    )


def solution(mesh):
    placed = (
        P(None, None, "gx", "gy"),
        P(None, ("gx", "gy")),
        P(None, ("gx", "gy")),
        P(None, ("gx", "gy")),
        P(None, ("gx", "gy")),
        P(None, None, ("gx", "gy")),
        P(("gx", "gy")),
        P(("gx", "gy"), None, None),
        P(("gx", "gy"), None),
    )
    return jax.shard_map(
        on_device,
        mesh=mesh,
        in_specs=placed,
        out_specs=(
            P(None, ("gx", "gy")),
            P(None, ("gx", "gy")),
            P(None, None, ("gx", "gy")),
            P(None, None, ("gx", "gy")),
            P(None, None, None, ("gx", "gy")),
        ),
        check_vma=False,
    )
```

```python
import functools

import jax
import jax.numpy as jnp
from jax import lax
from jax.experimental import pallas as pl
from jax.experimental.pallas import tpu as pltpu
from jax.sharding import PartitionSpec as P

neighbours = ((-1, -1), (-1, 0), (-1, 1), (0, -1), (0, 1), (1, -1), (1, 0), (1, 1))
step_dt = 0.1
relax_tau = 0.5
basset_coef = 0.3
MESH = pl.DeviceIdType.MESH
F32 = jnp.float32
BF16 = jnp.bfloat16


def basis_rows(s):
    return (
        -s * (s - 1.0) * (s - 2.0) / 6.0,
        (s + 1.0) * (s - 1.0) * (s - 2.0) / 2.0,
        -(s + 1.0) * s * (s - 2.0) / 2.0,
        (s + 1.0) * s * (s - 1.0) / 6.0,
    )


def pick_weight(d, w):
    out = jnp.where(d == 0, w[0], 0.0)
    for p in range(1, 4):
        out = jnp.where(d == p, w[p], out)
    return out


def split(v):
    hi = v.astype(BF16)
    return hi, (v - hi.astype(F32)).astype(BF16)


def iota(shape, dim):
    return lax.broadcasted_iota(jnp.int32, shape, dim)


def contract_lanes(a, b):
    return lax.dot_general(a, b, (((1,), (1,)), ((), ())), preferred_element_type=F32)


def main_kernel(
    sizes,
    live, counts, slots, cell, shift, frac, speed, flow, hist,
    res, rec_hist, rec_state, moved,
    i_cell, i_shift, i_frac, i_speed, i_slots, i_counts,
    f_buf, h_buf, a3, w3, sx, rx, ty, sy, ry, fl, sel, mslot, hhi, hlo, tail_s, s_hist, s_state,
    sem_i, sem_f, sem_h, sem_xs, sem_xr, sem_ys, sem_yr, sem_rs, sem_rr, sem_ss, sem_sr,
):
    nx, ny, nz, nb, cap, steps, gx_n, gy_n = sizes
    zx = nz * nx
    xh = 4 * nz
    half = 2 * nz
    k3 = 3 * zx
    chunk = 512
    m = 6 * ny
    gx = lax.axis_index("gx")
    gy = lax.axis_index("gy")
    wrap_x = lambda i: lax.rem(gx + i + gx_n, gx_n)
    wrap_y = lambda i: lax.rem(gy + i + gy_n, gy_n)

    def f_copy(c):
        return pltpu.make_async_copy(flow.at[c], f_buf.at[c], sem_f.at[c])

    def h_copy(c):
        return pltpu.make_async_copy(hist.at[c], h_buf.at[c], sem_h.at[c])

    small = [
        pltpu.make_async_copy(a, b, sem_i.at[i])
        for i, (a, b) in enumerate(
            (
                (cell, i_cell), (shift, i_shift), (frac, i_frac), (speed, i_speed),
                (slots, i_slots), (counts, i_counts),
            )
        )
    ]
    for c in range(6):
        f_copy(c).start()
    for cp in small:
        cp.start()
    for c in range(3):
        h_copy(c).start()

    barrier = pltpu.get_barrier_semaphore()
    for dx, dy in neighbours:
        pl.semaphore_signal(barrier, inc=1, device_id=(wrap_x(dx), wrap_y(dy)), device_id_type=MESH)
    sy[...] = jnp.zeros_like(sy)

    def pack_x(c, _):
        f_copy(c).wait()
        for z in range(nz):
            sx[0, c, 2 * z : 2 * z + 2, :] = f_buf[c, z, 0:2, :]
            sx[1, c, 2 * z : 2 * z + 2, :] = f_buf[c, z, nx - 2 : nx, :]
        return 0

    lax.fori_loop(0, 6, pack_x, 0)
    pl.semaphore_wait(barrier, 8)
    x_copies = [
        pltpu.make_async_remote_copy(
            src_ref=sx.at[side], dst_ref=rx.at[1 - side], send_sem=sem_xs.at[side],
            recv_sem=sem_xr.at[1 - side], device_id=(wrap_x(2 * side - 1), gy), device_id_type=MESH,
        )
        for side in range(2)
    ]
    for cp in x_copies:
        cp.start()

    def lanes_of(j):
        return pl.ds(pl.multiple_of(j * chunk, chunk), chunk)

    def weights(cells, shifts, fracs):
        base = cells + shifts
        w = basis_rows(fracs - shifts.astype(F32))

        def along(pos, dim):
            d = pos - base[dim : dim + 1] + 1
            if dim == 2:
                d = jnp.where(d < 0, d + nz, jnp.where(d >= nz, d - nz, d))
            return pick_weight(d, [v[dim : dim + 1] for v in w])

        return along

    def build_w(cols, width, along):
        wx = along(iota((nx, width), 0), 0)
        wz = along(iota((nz, width), 0), 2)
        for z in range(nz):
            hi, lo = split(wx * wz[z : z + 1])
            w3[z * nx : (z + 1) * nx, cols] = hi
            w3[zx + z * nx : zx + (z + 1) * nx, cols] = hi
            w3[2 * zx + z * nx : 2 * zx + (z + 1) * nx, cols] = lo
        r = iota((xh, width), 0)
        far = r >= half
        q = jnp.where(far, r - half, r)
        hi, lo = split(along(jnp.where(far, nx, -2) + (q & 1), 0) * along(q >> 1, 2))
        w3[k3 : k3 + xh, cols] = hi
        w3[k3 + xh : k3 + 2 * xh, cols] = hi
        w3[k3 + 2 * xh : k3 + 3 * xh, cols] = lo
        w3[k3 + 3 * xh : k3 + 4 * xh, cols] = jnp.zeros_like(lo)

    def interpolate(cols, width, along):
        p = jnp.dot(a3[...], w3[:, cols], preferred_element_type=F32)
        wy = along(iota((ny, width), 0), 1)
        inner = jnp.sum(p[0:m].reshape(6, ny, width) * wy[None], axis=1)
        wyh = [along(y, 1) for y in (-2, -1, ny, ny + 1)]
        outer = []
        for c in range(6):
            at = m + 2 * c
            extra = p[at : at + 1] * wyh[0] + p[at + 1 : at + 2] * wyh[1]
            at += 16
            outer.append(extra + p[at : at + 1] * wyh[2] + p[at + 1 : at + 2] * wyh[3])
        return inner + jnp.concatenate(outer, axis=0)

    def advance(fluid, v0, fracs, tail):
        fluid_u = fluid[0:3]
        fluid_a = fluid[3:6]

        def rate(v):
            return 3.0 * fluid_a + (fluid_u - v) / relax_tau + basset_coef * (fluid_u - v + tail)

        v1 = v0 + step_dt * rate(v0)
        v2 = 0.75 * v0 + 0.25 * (v1 + step_dt * rate(v1))
        vn = v0 / 3.0 + 2.0 / 3.0 * (v2 + step_dt * rate(v2))
        posn = fracs + step_dt * (v0 / 6.0 + v1 / 6.0 + 2.0 * v2 / 3.0)
        return vn, posn, fluid_u - vn

    def rows_of(c):
        return pl.ds(pl.multiple_of(c * ny, ny), ny)

    def turn(c, _):
        t = jnp.transpose(f_buf[c].reshape(zx, ny))
        hi, lo = split(t)
        rows = rows_of(c)
        a3[rows, 0:zx] = hi
        a3[rows, zx : 2 * zx] = lo
        a3[rows, 2 * zx : 3 * zx] = hi
        ty[c, 0:2, 0:zx] = t[0:2]
        ty[c, 2:4, 0:zx] = t[ny - 2 : ny]
        return 0

    lax.fori_loop(0, 6, turn, 0)

    for cp in x_copies:
        cp.wait()

    def turn_x(c, _):
        block = jnp.concatenate([rx[0, c], rx[1, c], jnp.zeros((ny - xh, ny), F32)], axis=0)
        t = jnp.transpose(block)
        ty[c, 0:2, zx : zx + ny] = t[0:2]
        ty[c, 2:4, zx : zx + ny] = t[ny - 2 : ny]
        hi = t.astype(BF16).astype(F32)
        lo = t - hi
        rows = rows_of(c)
        a3[rows, k3 : k3 + ny] = (hi + pltpu.roll(lo, xh, 1)).astype(BF16)
        a3[rows, k3 + ny : k3 + 2 * ny] = hi.astype(BF16)
        return 0

    lax.fori_loop(0, 6, turn_x, 0)
    for c in range(6):
        sy[0, 2 * c : 2 * c + 2, :] = ty[c, 0:2, :]
        sy[1, 2 * c : 2 * c + 2, :] = ty[c, 2:4, :]
    y_copies = [
        pltpu.make_async_remote_copy(
            src_ref=sy.at[side], dst_ref=ry.at[1 - side], send_sem=sem_ys.at[side],
            recv_sem=sem_yr.at[1 - side], device_id=(gx, wrap_y(2 * side - 1)), device_id_type=MESH,
        )
        for side in range(2)
    ]
    for cp in y_copies:
        cp.start()

    for cp in small:
        cp.wait()

    mslot[...] = jnp.zeros_like(mslot)
    mslot[0:8, 0:cap] = i_slots[0].astype(F32)
    cols_t = jnp.transpose(mslot[...])
    for d in range(8):
        col = cols_t[0:cap, d : d + 1]
        col = jnp.where(iota((cap, 1), 0) < i_counts[0, d], col, -1.0).astype(jnp.int32)
        sel[d * cap : (d + 1) * cap, :] = (iota((cap, nb), 1) == col).astype(F32).astype(BF16)
    karg = iota((steps, 128), 0).astype(F32) + 1.0
    quad = (jnp.sqrt(karg + 1.0) - jnp.sqrt(karg))[:, 0:1]

    def pick_history(c, _):
        h_copy(c).wait()
        h = h_buf[c]
        tail_s[c] = jnp.sum(h * quad, axis=0, keepdims=True)
        hi, lo = split(h)
        hhi[...] = hi
        hlo[...] = lo
        picked = contract_lanes(sel[...], hhi[...]) + contract_lanes(sel[...], hlo[...])
        picked = pltpu.roll(picked, 1, 1)
        s_hist[:, :, pl.ds(pl.multiple_of(c * steps, steps), steps)] = picked.reshape(8, cap, steps)
        return 0

    lax.fori_loop(0, 3, pick_history, 0)
    r_copies = [
        pltpu.make_async_remote_copy(
            src_ref=s_hist.at[d], dst_ref=rec_hist.at[d], send_sem=sem_rs.at[d],
            recv_sem=sem_rr.at[d], device_id=(wrap_x(dx), wrap_y(dy)), device_id_type=MESH,
        )
        for d, (dx, dy) in enumerate(neighbours)
    ]
    for cp in r_copies:
        cp.start()

    leaving = 8 * cap
    tail = jnp.concatenate([tail_s[c] for c in range(3)], axis=0)
    own = jnp.concatenate(
        [
            i_cell[...].astype(F32), i_shift[...].astype(F32), i_frac[...], i_speed[...], tail,
            jnp.ones((1, nb), F32),
        ],
        axis=0,
    )
    hi, lo = split(own)
    own = contract_lanes(hi, sel[...]) + contract_lanes(lo, sel[...])
    lv_cols = slice(nb, nb + leaving)
    lv_along = weights(own[0:3].astype(jnp.int32), own[3:6].astype(jnp.int32), own[6:9])
    build_w(lv_cols, leaving, lv_along)

    def chunk_weights(cols):
        return weights(i_cell[:, cols], i_shift[:, cols], i_frac[:, cols])

    def build_chunk(j, _):
        cols = lanes_of(j)
        build_w(cols, chunk, chunk_weights(cols))
        return 0

    lax.fori_loop(0, nb // chunk, build_chunk, 0)

    for cp in y_copies:
        cp.wait()
    for side in range(2):
        rows = slice(m + 16 * side, m + 16 * side + 16)
        v = ry[side]
        hi, lo = split(v[:, 0:zx])
        a3[rows, 0:zx] = hi
        a3[rows, zx : 2 * zx] = lo
        a3[rows, 2 * zx : 3 * zx] = hi
        t = v[:, zx : zx + ny]
        thi = t.astype(BF16).astype(F32)
        a3[rows, k3 : k3 + ny] = (thi + pltpu.roll(t - thi, xh, 1)).astype(BF16)
        a3[rows, k3 + ny : k3 + 2 * ny] = thi.astype(BF16)

    lv = advance(interpolate(lv_cols, leaving, lv_along), own[9:12], own[6:9], own[12:15])
    used = own[15:16] > 0.5
    mslot[...] = jnp.zeros_like(mslot)
    for i, v in enumerate(lv):
        mslot[3 * i : 3 * i + 3, :] = jnp.where(used, v, 0.0)
    s_state[...] = jnp.transpose(mslot[...]).reshape(8, cap, 128)
    s_copies = [
        pltpu.make_async_remote_copy(
            src_ref=s_state.at[d], dst_ref=rec_state.at[d], send_sem=sem_ss.at[d],
            recv_sem=sem_sr.at[d], device_id=(wrap_x(dx), wrap_y(dy)), device_id_type=MESH,
        )
        for d, (dx, dy) in enumerate(neighbours)
    ]
    for cp in s_copies:
        cp.start()

    def chunk_fluid(j, _):
        cols = lanes_of(j)
        fl[0:6, cols] = interpolate(cols, chunk, chunk_weights(cols))
        return 0

    lax.fori_loop(0, nb // chunk, chunk_fluid, 0)

    keep = iota((3, nb), 1) < live[0]
    for i, v in enumerate(advance(fl[0:6, :], i_speed[...], i_frac[...], tail)):
        res[3 * i : 3 * i + 3, :] = jnp.where(keep, v, 0.0)
    res[9:16, :] = jnp.zeros((7, nb), F32)

    for c in range(3):
        fl[c : c + 1, :] = res[6 + c : 7 + c, :]

    def move(i, _):
        cols = pl.ds(pl.multiple_of(i * 128, 128), 128)
        alive = (iota((1, 128), 1) + i * 128) < live[0]
        top = fl[:, cols]
        for c in range(3):
            h = pltpu.roll(h_buf[c, :, cols], 1, 0)
            h = jnp.where(iota((steps, 128), 0) == 0, top[c : c + 1], h)
            moved[c, :, cols] = jnp.where(alive, h, 0.0)
        return 0

    lax.fori_loop(0, nb // 128, move, 0)
    for cp in r_copies + s_copies:
        cp.wait()


def finish_kernel(
    cap, steps,
    res, rec_hist, rec_state, moved,
    vn, posn, out_hist, arr_state, arr_hist,
    b_vn, b_posn, b_state, b_hist, sems,
):
    copies = [pltpu.make_async_copy(moved, out_hist, sems.at[0])]
    copies[0].start()

    def send(src, dst):
        cp = pltpu.make_async_copy(src, dst, sems.at[len(copies)])
        cp.start()
        copies.append(cp)

    b_vn[...] = res[0:3, :]
    send(b_vn, vn)
    b_posn[...] = res[3:6, :]
    send(b_posn, posn)
    t = jnp.transpose(rec_state[...].reshape(8 * cap, 128))
    for d in range(8):
        b_state[:, d, :] = t[0:6, d * cap : (d + 1) * cap]
    send(b_state, arr_state)
    first = iota((cap, steps), 1) == 0
    for d in range(8):
        for c in range(3):
            col = rec_state[d, :, 6 + c : 7 + c]
            b_hist[d, c] = jnp.where(first, col, rec_hist[d, :, c * steps : (c + 1) * steps])
    send(b_hist, arr_hist)
    for cp in copies:
        cp.wait()


def on_device(flow, cell, shift, frac, speed, hist, live, slots, counts):
    _, nz, nx, ny = flow.shape
    nb = speed.shape[1]
    steps = hist.shape[1]
    cap = slots.shape[2]
    zx = nz * nx
    k3 = 3 * zx + 4 * 4 * nz
    sizes = (nx, ny, nz, nb, cap, steps, lax.axis_size("gx"), lax.axis_size("gy"))
    vmem = pl.BlockSpec(memory_space=pltpu.VMEM)
    hbm = pl.BlockSpec(memory_space=pltpu.HBM)
    dma = pltpu.SemaphoreType.DMA
    I32 = jnp.int32
    inputs = (counts, slots, cell, shift, frac, speed, flow, hist)
    gathered = pl.pallas_call(
        functools.partial(main_kernel, sizes),
        out_shape=(
            jax.ShapeDtypeStruct((16, nb), F32),
            jax.ShapeDtypeStruct((8, cap, 3 * steps), F32),
            jax.ShapeDtypeStruct((8, cap, 128), F32),
            jax.ShapeDtypeStruct((3, steps, nb), F32),
        ),
        in_specs=[pl.BlockSpec(memory_space=pltpu.SMEM)] + [hbm] * 8,
        out_specs=[vmem] * 4,
        scratch_shapes=[
            pltpu.VMEM((3, nb), I32),
            pltpu.VMEM((3, nb), I32),
            pltpu.VMEM((3, nb), F32),
            pltpu.VMEM((3, nb), F32),
            pltpu.VMEM((1, 8, cap), I32),
            pltpu.SMEM((1, 8), I32),
            pltpu.VMEM((6, nz, nx, ny), F32),
            pltpu.VMEM((3, steps, nb), F32),
            pltpu.VMEM((6 * ny + 32, k3), BF16),
            pltpu.VMEM((k3, nb + 8 * cap), BF16),
            pltpu.VMEM((2, 6, 2 * nz, ny), F32),
            pltpu.VMEM((2, 6, 2 * nz, ny), F32),
            pltpu.VMEM((6, 8, zx + ny), F32),
            pltpu.VMEM((2, 16, zx + ny), F32),
            pltpu.VMEM((2, 16, zx + ny), F32),
            pltpu.VMEM((8, nb), F32),
            pltpu.VMEM((8 * cap, nb), BF16),
            pltpu.VMEM((128, 128), F32),
            pltpu.VMEM((steps, nb), BF16),
            pltpu.VMEM((steps, nb), BF16),
            pltpu.VMEM((3, 1, nb), F32),
            pltpu.VMEM((8, cap, 3 * steps), F32),
            pltpu.VMEM((8, cap, 128), F32),
            dma((6,)), dma((6,)), dma((3,)), dma((2,)), dma((2,)), dma((2,)), dma((2,)),
            dma((8,)), dma((8,)), dma((8,)), dma((8,)),
        ],
        compiler_params=pltpu.CompilerParams(
            collective_id=0, has_side_effects=True, vmem_limit_bytes=44 * 2**20
        ),
        name="interpolate_and_migrate",
    )(live, *(pltpu.with_memory_space_constraint(v, pltpu.HBM) for v in inputs))

    vn, posn, out_hist, arr_state, arr_hist = pl.pallas_call(
        functools.partial(finish_kernel, cap, steps),
        out_shape=(
            jax.ShapeDtypeStruct((3, nb), F32),
            jax.ShapeDtypeStruct((3, nb), F32),
            jax.ShapeDtypeStruct((3, steps, nb), F32),
            jax.ShapeDtypeStruct((6, 8, cap), F32),
            jax.ShapeDtypeStruct((8, 3, cap, steps), F32),
        ),
        in_specs=[vmem] * 4,
        out_specs=[hbm] * 5,
        scratch_shapes=[
            pltpu.VMEM((3, nb), F32),
            pltpu.VMEM((3, nb), F32),
            pltpu.VMEM((6, 8, cap), F32),
            pltpu.VMEM((8, 3, cap, steps), F32),
            dma((5,)),
        ],
        compiler_params=pltpu.CompilerParams(vmem_limit_bytes=32 * 2**20),
        name="write_results",
    )(*gathered)
    return (
        vn,
        posn,
        out_hist,
        jnp.transpose(arr_state, (1, 0, 2)),
        jnp.transpose(arr_hist, (0, 1, 3, 2)),
    )


def solution(mesh):
    placed = (
        P(None, None, "gx", "gy"),
        P(None, ("gx", "gy")),
        P(None, ("gx", "gy")),
        P(None, ("gx", "gy")),
        P(None, ("gx", "gy")),
        P(None, None, ("gx", "gy")),
        P(("gx", "gy")),
        P(("gx", "gy"), None, None),
        P(("gx", "gy"), None),
    )
    return jax.shard_map(
        on_device,
        mesh=mesh,
        in_specs=placed,
        out_specs=(
            P(None, ("gx", "gy")),
            P(None, ("gx", "gy")),
            P(None, None, ("gx", "gy")),
            P(None, None, ("gx", "gy")),
            P(None, None, None, ("gx", "gy")),
        ),
        check_vma=False,
    )
```

```python
import functools

import jax
import jax.numpy as jnp
from jax import lax
from jax.experimental import pallas as pl
from jax.experimental.pallas import tpu as pltpu
from jax.sharding import PartitionSpec as P

neighbours = ((-1, -1), (-1, 0), (-1, 1), (0, -1), (0, 1), (1, -1), (1, 0), (1, 1))
step_dt = 0.1
relax_tau = 0.5
basset_coef = 0.3
MESH = pl.DeviceIdType.MESH
F32 = jnp.float32
BF16 = jnp.bfloat16


def basis_rows(s):
    return (
        -s * (s - 1.0) * (s - 2.0) / 6.0,
        (s + 1.0) * (s - 1.0) * (s - 2.0) / 2.0,
        -(s + 1.0) * s * (s - 2.0) / 2.0,
        (s + 1.0) * s * (s - 1.0) / 6.0,
    )


def pick_weight(d, w):
    out = jnp.where(d == 0, w[0], 0.0)
    for p in range(1, 4):
        out = jnp.where(d == p, w[p], out)
    return out


def split(v):
    hi = v.astype(BF16)
    return hi, (v - hi.astype(F32)).astype(BF16)


def iota(shape, dim):
    return lax.broadcasted_iota(jnp.int32, shape, dim)


def contract_lanes(a, b):
    return lax.dot_general(a, b, (((1,), (1,)), ((), ())), preferred_element_type=F32)


def main_kernel(
    sizes,
    live, counts, slots, cell, shift, frac, speed, flow, hist,
    res, rec_hist, rec_state, moved,
    i_cell, i_shift, i_frac, i_speed, i_slots, i_counts,
    f_buf, h_buf, a3, w_lv, w3, sx, rx, ty, sy, ry, fl, sel, mslot, hhi, hlo, tail_s, s_hist, s_state,
    sem_i, sem_f, sem_h, sem_xs, sem_xr, sem_ys, sem_yr, sem_rs, sem_rr, sem_ss, sem_sr,
):
    nx, ny, nz, nb, cap, steps, chunk, gx_n, gy_n = sizes
    zx = nz * nx
    xh = 4 * nz
    half = 2 * nz
    k3 = 3 * zx
    m = 6 * ny
    gx = lax.axis_index("gx")
    gy = lax.axis_index("gy")
    wrap_x = lambda i: lax.rem(gx + i + gx_n, gx_n)
    wrap_y = lambda i: lax.rem(gy + i + gy_n, gy_n)

    def f_copy(c):
        return pltpu.make_async_copy(flow.at[c], f_buf.at[c], sem_f.at[c])

    def h_copy(c):
        return pltpu.make_async_copy(hist.at[c], h_buf.at[c], sem_h.at[c])

    small = [
        pltpu.make_async_copy(a, b, sem_i.at[i])
        for i, (a, b) in enumerate(
            (
                (cell, i_cell), (shift, i_shift), (frac, i_frac), (speed, i_speed),
                (slots, i_slots), (counts, i_counts),
            )
        )
    ]
    for c in range(6):
        f_copy(c).start()
    for cp in small:
        cp.start()
    for c in range(3):
        h_copy(c).start()

    barrier = pltpu.get_barrier_semaphore()
    for dx, dy in neighbours:
        pl.semaphore_signal(barrier, inc=1, device_id=(wrap_x(dx), wrap_y(dy)), device_id_type=MESH)
    sy[...] = jnp.zeros_like(sy)

    def pack_x(c, _):
        f_copy(c).wait()
        for z in range(nz):
            sx[0, c, 2 * z : 2 * z + 2, :] = f_buf[c, z, 0:2, :]
            sx[1, c, 2 * z : 2 * z + 2, :] = f_buf[c, z, nx - 2 : nx, :]
        return 0

    lax.fori_loop(0, 6, pack_x, 0)
    pl.semaphore_wait(barrier, 8)
    x_copies = [
        pltpu.make_async_remote_copy(
            src_ref=sx.at[side], dst_ref=rx.at[1 - side], send_sem=sem_xs.at[side],
            recv_sem=sem_xr.at[1 - side], device_id=(wrap_x(2 * side - 1), gy), device_id_type=MESH,
        )
        for side in range(2)
    ]
    for cp in x_copies:
        cp.start()

    def weights(cells, shifts, fracs):
        base = cells + shifts
        w = basis_rows(fracs - shifts.astype(F32))

        def along(pos, dim):
            d = pos - base[dim : dim + 1] + 1
            if dim == 2:
                d = jnp.where(d < 0, d + nz, jnp.where(d >= nz, d - nz, d))
            return pick_weight(d, [v[dim : dim + 1] for v in w])

        return along

    def build_w(w3, width, along):
        wx = along(iota((nx, width), 0), 0)
        wz = along(iota((nz, width), 0), 2)
        for z in range(nz):
            hi, lo = split(wx * wz[z : z + 1])
            w3[z * nx : (z + 1) * nx] = hi
            w3[zx + z * nx : zx + (z + 1) * nx] = hi
            w3[2 * zx + z * nx : 2 * zx + (z + 1) * nx] = lo
        r = iota((xh, width), 0)
        far = r >= half
        q = jnp.where(far, r - half, r)
        hi, lo = split(along(jnp.where(far, nx, -2) + (q & 1), 0) * along(q >> 1, 2))
        w3[k3 : k3 + xh] = hi
        w3[k3 + xh : k3 + 2 * xh] = hi
        w3[k3 + 2 * xh : k3 + 3 * xh] = lo
        w3[k3 + 3 * xh : k3 + 4 * xh] = jnp.zeros_like(lo)

    def interpolate(w3, width, along):
        p = jnp.dot(a3[...], w3[...], preferred_element_type=F32)
        wy = along(iota((ny, width), 0), 1)
        inner = jnp.sum(p[0:m].reshape(6, ny, width) * wy[None], axis=1)
        wyh = [along(y, 1) for y in (-2, -1, ny, ny + 1)]
        outer = []
        for c in range(6):
            at = m + 2 * c
            extra = p[at : at + 1] * wyh[0] + p[at + 1 : at + 2] * wyh[1]
            at += 16
            outer.append(extra + p[at : at + 1] * wyh[2] + p[at + 1 : at + 2] * wyh[3])
        return inner + jnp.concatenate(outer, axis=0)

    def advance(fluid, v0, fracs, tail):
        fluid_u = fluid[0:3]
        fluid_a = fluid[3:6]

        def rate(v):
            return 3.0 * fluid_a + (fluid_u - v) / relax_tau + basset_coef * (fluid_u - v + tail)

        v1 = v0 + step_dt * rate(v0)
        v2 = 0.75 * v0 + 0.25 * (v1 + step_dt * rate(v1))
        vn = v0 / 3.0 + 2.0 / 3.0 * (v2 + step_dt * rate(v2))
        posn = fracs + step_dt * (v0 / 6.0 + v1 / 6.0 + 2.0 * v2 / 3.0)
        return vn, posn, fluid_u - vn

    for c in range(6):
        t = jnp.transpose(f_buf[c].reshape(zx, ny))
        hi, lo = split(t)
        rows = slice(c * ny, (c + 1) * ny)
        a3[rows, 0:zx] = hi
        a3[rows, zx : 2 * zx] = lo
        a3[rows, 2 * zx : 3 * zx] = hi
        ty[c, 0:2, 0:zx] = t[0:2]
        ty[c, 2:4, 0:zx] = t[ny - 2 : ny]

    for cp in x_copies:
        cp.wait()

    for c in range(6):
        block = jnp.concatenate([rx[0, c], rx[1, c], jnp.zeros((ny - xh, ny), F32)], axis=0)
        t = jnp.transpose(block)
        ty[c, 0:2, zx : zx + ny] = t[0:2]
        ty[c, 2:4, zx : zx + ny] = t[ny - 2 : ny]
        hi = t.astype(BF16).astype(F32)
        lo = t - hi
        rows = slice(c * ny, (c + 1) * ny)
        a3[rows, k3 : k3 + ny] = (hi + pltpu.roll(lo, xh, 1)).astype(BF16)
        a3[rows, k3 + ny : k3 + 2 * ny] = hi.astype(BF16)
    for c in range(6):
        sy[0, 2 * c : 2 * c + 2, :] = ty[c, 0:2, :]
        sy[1, 2 * c : 2 * c + 2, :] = ty[c, 2:4, :]
    y_copies = [
        pltpu.make_async_remote_copy(
            src_ref=sy.at[side], dst_ref=ry.at[1 - side], send_sem=sem_ys.at[side],
            recv_sem=sem_yr.at[1 - side], device_id=(gx, wrap_y(2 * side - 1)), device_id_type=MESH,
        )
        for side in range(2)
    ]
    for cp in y_copies:
        cp.start()

    for cp in small:
        cp.wait()

    mslot[...] = jnp.zeros_like(mslot)
    mslot[0:8, 0:cap] = i_slots[0].astype(F32)
    cols_t = jnp.transpose(mslot[...])
    for d in range(8):
        col = cols_t[0:cap, d : d + 1]
        col = jnp.where(iota((cap, 1), 0) < i_counts[0, d], col, -1.0).astype(jnp.int32)
        sel[d * cap : (d + 1) * cap, :] = (iota((cap, nb), 1) == col).astype(F32).astype(BF16)
    karg = iota((steps, 128), 0).astype(F32) + 1.0
    quad = (jnp.sqrt(karg + 1.0) - jnp.sqrt(karg))[:, 0:1]

    alive = iota((1, nb), 1) < live[0]
    for c in range(3):
        h_copy(c).wait()
    for c in range(3):
        h = h_buf[c]
        tail_s[c] = jnp.sum(h * quad, axis=0, keepdims=True)
        hi, lo = split(h)
        hhi[c] = hi
        hlo[c] = lo
        picked = contract_lanes(sel[...], hhi[c]) + contract_lanes(sel[...], hlo[c])
        picked = pltpu.roll(picked, 1, 1)
        s_hist[:, :, c * steps : (c + 1) * steps] = picked.reshape(8, cap, steps)
        moved[c] = jnp.where(alive, pltpu.roll(h, 1, 0), 0.0)
    r_copies = [
        pltpu.make_async_remote_copy(
            src_ref=s_hist.at[d], dst_ref=rec_hist.at[d], send_sem=sem_rs.at[d],
            recv_sem=sem_rr.at[d], device_id=(wrap_x(dx), wrap_y(dy)), device_id_type=MESH,
        )
        for d, (dx, dy) in enumerate(neighbours)
    ]
    for cp in r_copies:
        cp.start()

    leaving = 8 * cap
    tail = jnp.concatenate([tail_s[c] for c in range(3)], axis=0)
    own = jnp.concatenate(
        [
            i_cell[...].astype(F32), i_shift[...].astype(F32), i_frac[...], i_speed[...], tail,
            jnp.ones((1, nb), F32),
        ],
        axis=0,
    )
    hi, lo = split(own)
    own = contract_lanes(hi, sel[...]) + contract_lanes(lo, sel[...])
    lv_along = weights(own[0:3].astype(jnp.int32), own[3:6].astype(jnp.int32), own[6:9])
    build_w(w_lv, leaving, lv_along)

    for cp in y_copies:
        cp.wait()
    for side in range(2):
        rows = slice(m + 16 * side, m + 16 * side + 16)
        v = ry[side]
        hi, lo = split(v[:, 0:zx])
        a3[rows, 0:zx] = hi
        a3[rows, zx : 2 * zx] = lo
        a3[rows, 2 * zx : 3 * zx] = hi
        t = v[:, zx : zx + ny]
        thi = t.astype(BF16).astype(F32)
        a3[rows, k3 : k3 + ny] = (thi + pltpu.roll(t - thi, xh, 1)).astype(BF16)
        a3[rows, k3 + ny : k3 + 2 * ny] = thi.astype(BF16)

    chunks = nb // chunk
    spans = [slice(j * chunk, (j + 1) * chunk) for j in range(chunks)]
    along = [weights(i_cell[:, g], i_shift[:, g], i_frac[:, g]) for g in spans]
    build_w(w3.at[0], chunk, along[0])
    lv = advance(interpolate(w_lv, leaving, lv_along), own[9:12], own[6:9], own[12:15])
    used = own[15:16] > 0.5
    mslot[...] = jnp.zeros_like(mslot)
    for i, v in enumerate(lv):
        mslot[3 * i : 3 * i + 3, :] = jnp.where(used, v, 0.0)
    s_state[...] = jnp.transpose(mslot[...]).reshape(8, cap, 128)
    s_copies = [
        pltpu.make_async_remote_copy(
            src_ref=s_state.at[d], dst_ref=rec_state.at[d], send_sem=sem_ss.at[d],
            recv_sem=sem_sr.at[d], device_id=(wrap_x(dx), wrap_y(dy)), device_id_type=MESH,
        )
        for d, (dx, dy) in enumerate(neighbours)
    ]
    for cp in s_copies:
        cp.start()

    for j in range(chunks):
        if j + 1 < chunks:
            build_w(w3.at[j + 1], chunk, along[j + 1])
        fl[0:6, spans[j]] = interpolate(w3.at[j], chunk, along[j])

    keep = iota((3, nb), 1) < live[0]
    for i, v in enumerate(advance(fl[0:6, :], i_speed[...], i_frac[...], tail)):
        res[3 * i : 3 * i + 3, :] = jnp.where(keep, v, 0.0)
    res[9:16, :] = jnp.zeros((7, nb), F32)

    for c in range(3):
        moved[c, 0:1, :] = res[6 + c : 7 + c, :]
    for cp in r_copies + s_copies:
        cp.wait()


def finish_kernel(
    cap, steps,
    res, rec_hist, rec_state, moved,
    vn, posn, out_hist, arr_state, arr_hist,
    b_vn, b_posn, b_state, b_hist, sems,
):
    copies = [pltpu.make_async_copy(moved, out_hist, sems.at[0])]
    copies[0].start()

    def send(src, dst):
        cp = pltpu.make_async_copy(src, dst, sems.at[len(copies)])
        cp.start()
        copies.append(cp)

    b_vn[...] = res[0:3, :]
    send(b_vn, vn)
    b_posn[...] = res[3:6, :]
    send(b_posn, posn)
    t = jnp.transpose(rec_state[...].reshape(8 * cap, 128))
    for d in range(8):
        b_state[:, d, :] = t[0:6, d * cap : (d + 1) * cap]
    send(b_state, arr_state)
    first = iota((cap, steps), 1) == 0
    for d in range(8):
        for c in range(3):
            col = rec_state[d, :, 6 + c : 7 + c]
            b_hist[d, c] = jnp.where(first, col, rec_hist[d, :, c * steps : (c + 1) * steps])
    send(b_hist, arr_hist)
    for cp in copies:
        cp.wait()


def on_device(flow, cell, shift, frac, speed, hist, live, slots, counts):
    _, nz, nx, ny = flow.shape
    nb = speed.shape[1]
    steps = hist.shape[1]
    cap = slots.shape[2]
    zx = nz * nx
    k3 = 3 * zx + 4 * 4 * nz
    chunk = 512
    sizes = (nx, ny, nz, nb, cap, steps, chunk, lax.axis_size("gx"), lax.axis_size("gy"))
    vmem = pl.BlockSpec(memory_space=pltpu.VMEM)
    hbm = pl.BlockSpec(memory_space=pltpu.HBM)
    dma = pltpu.SemaphoreType.DMA
    I32 = jnp.int32
    inputs = (counts, slots, cell, shift, frac, speed, flow, hist)
    gathered = pl.pallas_call(
        functools.partial(main_kernel, sizes),
        out_shape=(
            jax.ShapeDtypeStruct((16, nb), F32),
            jax.ShapeDtypeStruct((8, cap, 3 * steps), F32),
            jax.ShapeDtypeStruct((8, cap, 128), F32),
            jax.ShapeDtypeStruct((3, steps, nb), F32),
        ),
        in_specs=[pl.BlockSpec(memory_space=pltpu.SMEM)] + [hbm] * 8,
        out_specs=[vmem] * 4,
        scratch_shapes=[
            pltpu.VMEM((3, nb), I32),
            pltpu.VMEM((3, nb), I32),
            pltpu.VMEM((3, nb), F32),
            pltpu.VMEM((3, nb), F32),
            pltpu.VMEM((1, 8, cap), I32),
            pltpu.SMEM((1, 8), I32),
            pltpu.VMEM((6, nz, nx, ny), F32),
            pltpu.VMEM((3, steps, nb), F32),
            pltpu.VMEM((6 * ny + 32, k3), BF16),
            pltpu.VMEM((k3, 8 * cap), BF16),
            pltpu.VMEM((nb // chunk, k3, chunk), BF16),
            pltpu.VMEM((2, 6, 2 * nz, ny), F32),
            pltpu.VMEM((2, 6, 2 * nz, ny), F32),
            pltpu.VMEM((6, 8, zx + ny), F32),
            pltpu.VMEM((2, 16, zx + ny), F32),
            pltpu.VMEM((2, 16, zx + ny), F32),
            pltpu.VMEM((8, nb), F32),
            pltpu.VMEM((8 * cap, nb), BF16),
            pltpu.VMEM((128, 128), F32),
            pltpu.VMEM((3, steps, nb), BF16),
            pltpu.VMEM((3, steps, nb), BF16),
            pltpu.VMEM((3, 1, nb), F32),
            pltpu.VMEM((8, cap, 3 * steps), F32),
            pltpu.VMEM((8, cap, 128), F32),
            dma((6,)), dma((6,)), dma((3,)), dma((2,)), dma((2,)), dma((2,)), dma((2,)),
            dma((8,)), dma((8,)), dma((8,)), dma((8,)),
        ],
        compiler_params=pltpu.CompilerParams(
            collective_id=0, has_side_effects=True, vmem_limit_bytes=44 * 2**20
        ),
        name="interpolate_and_migrate",
    )(live, *(pltpu.with_memory_space_constraint(v, pltpu.HBM) for v in inputs))

    vn, posn, out_hist, arr_state, arr_hist = pl.pallas_call(
        functools.partial(finish_kernel, cap, steps),
        out_shape=(
            jax.ShapeDtypeStruct((3, nb), F32),
            jax.ShapeDtypeStruct((3, nb), F32),
            jax.ShapeDtypeStruct((3, steps, nb), F32),
            jax.ShapeDtypeStruct((6, 8, cap), F32),
            jax.ShapeDtypeStruct((8, 3, cap, steps), F32),
        ),
        in_specs=[vmem] * 4,
        out_specs=[hbm] * 5,
        scratch_shapes=[
            pltpu.VMEM((3, nb), F32),
            pltpu.VMEM((3, nb), F32),
            pltpu.VMEM((6, 8, cap), F32),
            pltpu.VMEM((8, 3, cap, steps), F32),
            dma((5,)),
        ],
        compiler_params=pltpu.CompilerParams(vmem_limit_bytes=32 * 2**20),
        name="write_results",
    )(*gathered)
    return (
        vn,
        posn,
        out_hist,
        jnp.transpose(arr_state, (1, 0, 2)),
        jnp.transpose(arr_hist, (0, 1, 3, 2)),
    )


def solution(mesh):
    placed = (
        P(None, None, "gx", "gy"),
        P(None, ("gx", "gy")),
        P(None, ("gx", "gy")),
        P(None, ("gx", "gy")),
        P(None, ("gx", "gy")),
        P(None, None, ("gx", "gy")),
        P(("gx", "gy")),
        P(("gx", "gy"), None, None),
        P(("gx", "gy"), None),
    )
    return jax.shard_map(
        on_device,
        mesh=mesh,
        in_specs=placed,
        out_specs=(
            P(None, ("gx", "gy")),
            P(None, ("gx", "gy")),
            P(None, None, ("gx", "gy")),
            P(None, None, ("gx", "gy")),
            P(None, None, None, ("gx", "gy")),
        ),
        check_vma=False,
    )
```

```python
import functools

import jax
import jax.numpy as jnp
from jax import lax
from jax.experimental import pallas as pl
from jax.experimental.pallas import tpu as pltpu
from jax.sharding import PartitionSpec as P

neighbours = ((-1, -1), (-1, 0), (-1, 1), (0, -1), (0, 1), (1, -1), (1, 0), (1, 1))
step_dt = 0.1
relax_tau = 0.5
basset_coef = 0.3
MESH = pl.DeviceIdType.MESH
F32 = jnp.float32
BF16 = jnp.bfloat16


def basis_rows(s):
    return (
        -s * (s - 1.0) * (s - 2.0) / 6.0,
        (s + 1.0) * (s - 1.0) * (s - 2.0) / 2.0,
        -(s + 1.0) * s * (s - 2.0) / 2.0,
        (s + 1.0) * s * (s - 1.0) / 6.0,
    )


def pick_weight(d, w):
    out = jnp.where(d == 0, w[0], 0.0)
    for p in range(1, 4):
        out = jnp.where(d == p, w[p], out)
    return out


def split(v):
    hi = v.astype(BF16)
    return hi, (v - hi.astype(F32)).astype(BF16)


def iota(shape, dim):
    return lax.broadcasted_iota(jnp.int32, shape, dim)


def contract_lanes(a, b):
    return lax.dot_general(a, b, (((1,), (1,)), ((), ())), preferred_element_type=F32)


def main_kernel(
    sizes,
    live, counts, slots, cell, shift, frac, speed, flow, hist,
    res, rec_hist, rec_state, moved,
    i_cell, i_shift, i_frac, i_speed, i_slots, i_counts,
    f_buf, h_buf, a3, w_lv, w3, sx, rx, sy, ry, sc, rc, ys, fl, sel, mslot, hhi, hlo, tail_s, s_hist, s_state,
    sem_i, sem_f, sem_h, sem_xs, sem_xr, sem_ys, sem_yr, sem_cs, sem_cr, sem_rs, sem_rr, sem_ss, sem_sr,
):
    nx, ny, nz, nb, cap, steps, chunk, gx_n, gy_n = sizes
    zx = nz * nx
    xh = 4 * nz
    half = 2 * nz
    k3 = 3 * zx
    m = 6 * ny
    gx = lax.axis_index("gx")
    gy = lax.axis_index("gy")
    wrap_x = lambda i: lax.rem(gx + i + gx_n, gx_n)
    wrap_y = lambda i: lax.rem(gy + i + gy_n, gy_n)

    def f_copy(c):
        return pltpu.make_async_copy(flow.at[c], f_buf.at[c], sem_f.at[c])

    def h_copy(c):
        return pltpu.make_async_copy(hist.at[c], h_buf.at[c], sem_h.at[c])

    small = [
        pltpu.make_async_copy(a, b, sem_i.at[i])
        for i, (a, b) in enumerate(
            (
                (cell, i_cell), (shift, i_shift), (frac, i_frac), (speed, i_speed),
                (slots, i_slots), (counts, i_counts),
            )
        )
    ]
    for c in range(6):
        f_copy(c).start()
    for cp in small:
        cp.start()
    for c in range(3):
        h_copy(c).start()

    barrier = pltpu.get_barrier_semaphore()
    for dx, dy in neighbours:
        pl.semaphore_signal(barrier, inc=1, device_id=(wrap_x(dx), wrap_y(dy)), device_id_type=MESH)
    ys[...] = jnp.zeros_like(ys)

    def y_copy(src, dst, sem_s, sem_r, side):
        return pltpu.make_async_remote_copy(
            src_ref=src.at[side], dst_ref=dst.at[1 - side], send_sem=sem_s.at[side],
            recv_sem=sem_r.at[1 - side], device_id=(gx, wrap_y(2 * side - 1)), device_id_type=MESH,
        )

    def pack_x(c, _):
        f_copy(c).wait()
        for z in range(nz):
            sx[0, c, 2 * z : 2 * z + 2, :] = f_buf[c, z, 0:2, :]
            sx[1, c, 2 * z : 2 * z + 2, :] = f_buf[c, z, nx - 2 : nx, :]
        return 0

    lax.fori_loop(0, 6, pack_x, 0)
    pl.semaphore_wait(barrier, 8)
    x_copies = [
        pltpu.make_async_remote_copy(
            src_ref=sx.at[side], dst_ref=rx.at[1 - side], send_sem=sem_xs.at[side],
            recv_sem=sem_xr.at[1 - side], device_id=(wrap_x(2 * side - 1), gy), device_id_type=MESH,
        )
        for side in range(2)
    ]
    for cp in x_copies:
        cp.start()

    def weights(cells, shifts, fracs):
        base = cells + shifts
        w = basis_rows(fracs - shifts.astype(F32))

        def along(pos, dim):
            d = pos - base[dim : dim + 1] + 1
            if dim == 2:
                d = jnp.where(d < 0, d + nz, jnp.where(d >= nz, d - nz, d))
            return pick_weight(d, [v[dim : dim + 1] for v in w])

        return along

    def build_w(w3, width, along):
        wx = along(iota((nx, width), 0), 0)
        wz = along(iota((nz, width), 0), 2)
        for z in range(nz):
            hi, lo = split(wx * wz[z : z + 1])
            w3[z * nx : (z + 1) * nx] = hi
            w3[zx + z * nx : zx + (z + 1) * nx] = hi
            w3[2 * zx + z * nx : 2 * zx + (z + 1) * nx] = lo
        r = iota((xh, width), 0)
        far = r >= half
        q = jnp.where(far, r - half, r)
        hi, lo = split(along(jnp.where(far, nx, -2) + (q & 1), 0) * along(q >> 1, 2))
        w3[k3 : k3 + xh] = hi
        w3[k3 + xh : k3 + 2 * xh] = hi
        w3[k3 + 2 * xh : k3 + 3 * xh] = lo
        w3[k3 + 3 * xh : k3 + 4 * xh] = jnp.zeros_like(lo)

    def product(lo_row, hi_row, w3):
        return jnp.dot(a3[lo_row:hi_row, :], w3[...], preferred_element_type=F32)

    def inner_sum(p, width, along):
        wy = along(iota((ny, width), 0), 1)
        return jnp.sum(p.reshape(6, ny, width) * wy[None], axis=1)

    def outer_sum(p, along):
        wyh = [along(y, 1) for y in (-2, -1, ny, ny + 1)]
        outer = []
        for c in range(6):
            at = 2 * c
            extra = p[at : at + 1] * wyh[0] + p[at + 1 : at + 2] * wyh[1]
            at += 16
            outer.append(extra + p[at : at + 1] * wyh[2] + p[at + 1 : at + 2] * wyh[3])
        return jnp.concatenate(outer, axis=0)

    def interpolate(w3, width, along):
        p = product(0, m + 32, w3)
        return inner_sum(p[0:m], width, along) + outer_sum(p[m:], along)

    def advance(fluid, v0, fracs, tail):
        fluid_u = fluid[0:3]
        fluid_a = fluid[3:6]

        def rate(v):
            return 3.0 * fluid_a + (fluid_u - v) / relax_tau + basset_coef * (fluid_u - v + tail)

        v1 = v0 + step_dt * rate(v0)
        v2 = 0.75 * v0 + 0.25 * (v1 + step_dt * rate(v1))
        vn = v0 / 3.0 + 2.0 / 3.0 * (v2 + step_dt * rate(v2))
        posn = fracs + step_dt * (v0 / 6.0 + v1 / 6.0 + 2.0 * v2 / 3.0)
        return vn, posn, fluid_u - vn

    for c in range(6):
        t = jnp.transpose(f_buf[c].reshape(zx, ny))
        hi, lo = split(t)
        rows = slice(c * ny, (c + 1) * ny)
        a3[rows, 0:zx] = hi
        a3[rows, zx : 2 * zx] = lo
        a3[rows, 2 * zx : 3 * zx] = hi
        pair = slice(2 * (c % 2), 2 * (c % 2) + 2)
        sy[0, c // 2, pair, :] = t[0:2]
        sy[1, c // 2, pair, :] = t[ny - 2 : ny]
    y_copies = [y_copy(sy, ry, sem_ys, sem_yr, side) for side in range(2)]
    for cp in y_copies:
        cp.start()

    for cp in x_copies:
        cp.wait()

    for c in range(6):
        block = jnp.concatenate([rx[0, c], rx[1, c], jnp.zeros((ny - xh, ny), F32)], axis=0)
        t = jnp.transpose(block)
        pair = slice(2 * (c % 2), 2 * (c % 2) + 2)
        sc[0, c // 2, pair, :] = t[0:2]
        sc[1, c // 2, pair, :] = t[ny - 2 : ny]
        hi = t.astype(BF16).astype(F32)
        lo = t - hi
        rows = slice(c * ny, (c + 1) * ny)
        a3[rows, k3 : k3 + ny] = (hi + pltpu.roll(lo, xh, 1)).astype(BF16)
        a3[rows, k3 + ny : k3 + 2 * ny] = hi.astype(BF16)
    c_copies = [y_copy(sc, rc, sem_cs, sem_cr, side) for side in range(2)]
    for cp in c_copies:
        cp.start()

    for cp in small:
        cp.wait()

    mslot[...] = jnp.zeros_like(mslot)
    mslot[0:8, 0:cap] = i_slots[0].astype(F32)
    cols_t = jnp.transpose(mslot[...])
    for d in range(8):
        col = cols_t[0:cap, d : d + 1]
        col = jnp.where(iota((cap, 1), 0) < i_counts[0, d], col, -1.0).astype(jnp.int32)
        sel[d * cap : (d + 1) * cap, :] = (iota((cap, nb), 1) == col).astype(F32).astype(BF16)
    karg = iota((steps, 128), 0).astype(F32) + 1.0
    quad = (jnp.sqrt(karg + 1.0) - jnp.sqrt(karg))[:, 0:1]

    alive = iota((1, nb), 1) < live[0]
    for c in range(3):
        h_copy(c).wait()
    for c in range(3):
        h = h_buf[c]
        tail_s[c] = jnp.sum(h * quad, axis=0, keepdims=True)
        hi, lo = split(h)
        hhi[c] = hi
        hlo[c] = lo
        picked = contract_lanes(sel[...], hhi[c]) + contract_lanes(sel[...], hlo[c])
        picked = pltpu.roll(picked, 1, 1)
        s_hist[:, :, c * steps : (c + 1) * steps] = picked.reshape(8, cap, steps)
        moved[c] = jnp.where(alive, pltpu.roll(h, 1, 0), 0.0)
    r_copies = [
        pltpu.make_async_remote_copy(
            src_ref=s_hist.at[d], dst_ref=rec_hist.at[d], send_sem=sem_rs.at[d],
            recv_sem=sem_rr.at[d], device_id=(wrap_x(dx), wrap_y(dy)), device_id_type=MESH,
        )
        for d, (dx, dy) in enumerate(neighbours)
    ]
    for cp in r_copies:
        cp.start()

    leaving = 8 * cap
    tail = jnp.concatenate([tail_s[c] for c in range(3)], axis=0)
    own = jnp.concatenate(
        [
            i_cell[...].astype(F32), i_shift[...].astype(F32), i_frac[...], i_speed[...], tail,
            jnp.ones((1, nb), F32),
        ],
        axis=0,
    )
    hi, lo = split(own)
    own = contract_lanes(hi, sel[...]) + contract_lanes(lo, sel[...])
    lv_along = weights(own[0:3].astype(jnp.int32), own[3:6].astype(jnp.int32), own[6:9])
    build_w(w_lv, leaving, lv_along)

    chunks = nb // chunk
    spans = [slice(j * chunk, (j + 1) * chunk) for j in range(chunks)]
    along = [weights(i_cell[:, g], i_shift[:, g], i_frac[:, g]) for g in spans]
    build_w(w3.at[0], chunk, along[0])
    for j in range(1, chunks):
        build_w(w3.at[j], chunk, along[j])
    fl[0:6, spans[0]] = inner_sum(product(0, m, w3.at[0]), chunk, along[0])

    for cp in y_copies + c_copies:
        cp.wait()
    for side in range(2):
        rows = slice(m + 16 * side, m + 16 * side + 16)
        for g in range(3):
            ys[side, 4 * g : 4 * g + 4, 0:zx] = ry[side, g]
            ys[side, 4 * g : 4 * g + 4, zx : zx + ny] = rc[side, g]
        v = ys[side]
        hi, lo = split(v[:, 0:zx])
        a3[rows, 0:zx] = hi
        a3[rows, zx : 2 * zx] = lo
        a3[rows, 2 * zx : 3 * zx] = hi
        t = v[:, zx : zx + ny]
        thi = t.astype(BF16).astype(F32)
        a3[rows, k3 : k3 + ny] = (thi + pltpu.roll(t - thi, xh, 1)).astype(BF16)
        a3[rows, k3 + ny : k3 + 2 * ny] = thi.astype(BF16)

    lv = advance(interpolate(w_lv, leaving, lv_along), own[9:12], own[6:9], own[12:15])
    used = own[15:16] > 0.5
    mslot[...] = jnp.zeros_like(mslot)
    for i, v in enumerate(lv):
        mslot[3 * i : 3 * i + 3, :] = jnp.where(used, v, 0.0)
    s_state[...] = jnp.transpose(mslot[...]).reshape(8, cap, 128)
    s_copies = [
        pltpu.make_async_remote_copy(
            src_ref=s_state.at[d], dst_ref=rec_state.at[d], send_sem=sem_ss.at[d],
            recv_sem=sem_sr.at[d], device_id=(wrap_x(dx), wrap_y(dy)), device_id_type=MESH,
        )
        for d, (dx, dy) in enumerate(neighbours)
    ]
    for cp in s_copies:
        cp.start()

    fl[0:6, spans[0]] += outer_sum(product(m, m + 32, w3.at[0]), along[0])
    for j in range(1, chunks):
        fl[0:6, spans[j]] = interpolate(w3.at[j], chunk, along[j])

    keep = iota((3, nb), 1) < live[0]
    for i, v in enumerate(advance(fl[0:6, :], i_speed[...], i_frac[...], tail)):
        res[3 * i : 3 * i + 3, :] = jnp.where(keep, v, 0.0)
    res[9:16, :] = jnp.zeros((7, nb), F32)

    for c in range(3):
        moved[c, 0:1, :] = res[6 + c : 7 + c, :]
    for cp in r_copies + s_copies:
        cp.wait()


def finish_kernel(
    cap, steps,
    res, rec_hist, rec_state, moved,
    vn, posn, out_hist, arr_state, arr_hist,
    b_vn, b_posn, b_state, b_hist, sems,
):
    copies = [pltpu.make_async_copy(moved, out_hist, sems.at[0])]
    copies[0].start()

    def send(src, dst):
        cp = pltpu.make_async_copy(src, dst, sems.at[len(copies)])
        cp.start()
        copies.append(cp)

    b_vn[...] = res[0:3, :]
    send(b_vn, vn)
    b_posn[...] = res[3:6, :]
    send(b_posn, posn)
    t = jnp.transpose(rec_state[...].reshape(8 * cap, 128))
    for d in range(8):
        b_state[:, d, :] = t[0:6, d * cap : (d + 1) * cap]
    send(b_state, arr_state)
    first = iota((cap, steps), 1) == 0
    for d in range(8):
        for c in range(3):
            col = rec_state[d, :, 6 + c : 7 + c]
            b_hist[d, c] = jnp.where(first, col, rec_hist[d, :, c * steps : (c + 1) * steps])
    send(b_hist, arr_hist)
    for cp in copies:
        cp.wait()


def on_device(flow, cell, shift, frac, speed, hist, live, slots, counts):
    _, nz, nx, ny = flow.shape
    nb = speed.shape[1]
    steps = hist.shape[1]
    cap = slots.shape[2]
    zx = nz * nx
    k3 = 3 * zx + 4 * 4 * nz
    chunk = 512
    sizes = (nx, ny, nz, nb, cap, steps, chunk, lax.axis_size("gx"), lax.axis_size("gy"))
    vmem = pl.BlockSpec(memory_space=pltpu.VMEM)
    hbm = pl.BlockSpec(memory_space=pltpu.HBM)
    dma = pltpu.SemaphoreType.DMA
    I32 = jnp.int32
    inputs = (counts, slots, cell, shift, frac, speed, flow, hist)
    gathered = pl.pallas_call(
        functools.partial(main_kernel, sizes),
        out_shape=(
            jax.ShapeDtypeStruct((16, nb), F32),
            jax.ShapeDtypeStruct((8, cap, 3 * steps), F32),
            jax.ShapeDtypeStruct((8, cap, 128), F32),
            jax.ShapeDtypeStruct((3, steps, nb), F32),
        ),
        in_specs=[pl.BlockSpec(memory_space=pltpu.SMEM)] + [hbm] * 8,
        out_specs=[vmem] * 4,
        scratch_shapes=[
            pltpu.VMEM((3, nb), I32),
            pltpu.VMEM((3, nb), I32),
            pltpu.VMEM((3, nb), F32),
            pltpu.VMEM((3, nb), F32),
            pltpu.VMEM((1, 8, cap), I32),
            pltpu.SMEM((1, 8), I32),
            pltpu.VMEM((6, nz, nx, ny), F32),
            pltpu.VMEM((3, steps, nb), F32),
            pltpu.VMEM((6 * ny + 32, k3), BF16),
            pltpu.VMEM((k3, 8 * cap), BF16),
            pltpu.VMEM((nb // chunk, k3, chunk), BF16),
            pltpu.VMEM((2, 6, 2 * nz, ny), F32),
            pltpu.VMEM((2, 6, 2 * nz, ny), F32),
            pltpu.VMEM((2, 3, 4, zx), F32),
            pltpu.VMEM((2, 3, 4, zx), F32),
            pltpu.VMEM((2, 3, 4, ny), F32),
            pltpu.VMEM((2, 3, 4, ny), F32),
            pltpu.VMEM((2, 16, zx + ny), F32),
            pltpu.VMEM((8, nb), F32),
            pltpu.VMEM((8 * cap, nb), BF16),
            pltpu.VMEM((128, 128), F32),
            pltpu.VMEM((3, steps, nb), BF16),
            pltpu.VMEM((3, steps, nb), BF16),
            pltpu.VMEM((3, 1, nb), F32),
            pltpu.VMEM((8, cap, 3 * steps), F32),
            pltpu.VMEM((8, cap, 128), F32),
            dma((6,)), dma((6,)), dma((3,)), dma((2,)), dma((2,)), dma((2,)), dma((2,)),
            dma((2,)), dma((2,)),
            dma((8,)), dma((8,)), dma((8,)), dma((8,)),
        ],
        compiler_params=pltpu.CompilerParams(
            collective_id=0, has_side_effects=True, vmem_limit_bytes=44 * 2**20
        ),
        name="interpolate_and_migrate",
    )(live, *(pltpu.with_memory_space_constraint(v, pltpu.HBM) for v in inputs))

    vn, posn, out_hist, arr_state, arr_hist = pl.pallas_call(
        functools.partial(finish_kernel, cap, steps),
        out_shape=(
            jax.ShapeDtypeStruct((3, nb), F32),
            jax.ShapeDtypeStruct((3, nb), F32),
            jax.ShapeDtypeStruct((3, steps, nb), F32),
            jax.ShapeDtypeStruct((6, 8, cap), F32),
            jax.ShapeDtypeStruct((8, 3, cap, steps), F32),
        ),
        in_specs=[vmem] * 4,
        out_specs=[hbm] * 5,
        scratch_shapes=[
            pltpu.VMEM((3, nb), F32),
            pltpu.VMEM((3, nb), F32),
            pltpu.VMEM((6, 8, cap), F32),
            pltpu.VMEM((8, 3, cap, steps), F32),
            dma((5,)),
        ],
        compiler_params=pltpu.CompilerParams(vmem_limit_bytes=32 * 2**20),
        name="write_results",
    )(*gathered)
    return (
        vn,
        posn,
        out_hist,
        jnp.transpose(arr_state, (1, 0, 2)),
        jnp.transpose(arr_hist, (0, 1, 3, 2)),
    )


def solution(mesh):
    placed = (
        P(None, None, "gx", "gy"),
        P(None, ("gx", "gy")),
        P(None, ("gx", "gy")),
        P(None, ("gx", "gy")),
        P(None, ("gx", "gy")),
        P(None, None, ("gx", "gy")),
        P(("gx", "gy")),
        P(("gx", "gy"), None, None),
        P(("gx", "gy"), None),
    )
    return jax.shard_map(
        on_device,
        mesh=mesh,
        in_specs=placed,
        out_specs=(
            P(None, ("gx", "gy")),
            P(None, ("gx", "gy")),
            P(None, None, ("gx", "gy")),
            P(None, None, ("gx", "gy")),
            P(None, None, None, ("gx", "gy")),
        ),
        check_vma=False,
    )
```

```python
import functools

import jax
import jax.numpy as jnp
from jax import lax
from jax.experimental import pallas as pl
from jax.experimental.pallas import tpu as pltpu
from jax.sharding import PartitionSpec as P

neighbours = ((-1, -1), (-1, 0), (-1, 1), (0, -1), (0, 1), (1, -1), (1, 0), (1, 1))
step_dt = 0.1
relax_tau = 0.5
basset_coef = 0.3
MESH = pl.DeviceIdType.MESH
F32 = jnp.float32
BF16 = jnp.bfloat16


def basis_rows(s):
    return (
        -s * (s - 1.0) * (s - 2.0) / 6.0,
        (s + 1.0) * (s - 1.0) * (s - 2.0) / 2.0,
        -(s + 1.0) * s * (s - 2.0) / 2.0,
        (s + 1.0) * s * (s - 1.0) / 6.0,
    )


def pick_weight(d, w):
    out = jnp.where(d == 0, w[0], 0.0)
    for p in range(1, 4):
        out = jnp.where(d == p, w[p], out)
    return out


def split(v):
    hi = v.astype(BF16)
    return hi, (v - hi.astype(F32)).astype(BF16)


def iota(shape, dim):
    return lax.broadcasted_iota(jnp.int32, shape, dim)


def contract_lanes(a, b):
    return lax.dot_general(a, b, (((1,), (1,)), ((), ())), preferred_element_type=F32)


def main_kernel(
    sizes,
    live, counts, slots, cell, shift, frac, speed, flow, hist,
    res, rec_hist, rec_state, moved,
    i_cell, i_shift, i_frac, i_speed, i_slots, i_counts,
    f_buf, h_buf, a3, w_lv, w3, sx, rx, sy, ry, sc, rc, ys, fl, sel, mslot, hhi, hlo, tail_s, s_hist, s_state,
    sem_i, sem_f, sem_h, sem_xs, sem_xr, sem_ys, sem_yr, sem_cs, sem_cr, sem_rs, sem_rr, sem_ss, sem_sr,
):
    nx, ny, nz, nb, cap, steps, chunk, gx_n, gy_n = sizes
    zx = nz * nx
    xh = 4 * nz
    half = 2 * nz
    k3 = 3 * zx
    m = 6 * ny
    gx = lax.axis_index("gx")
    gy = lax.axis_index("gy")
    wrap_x = lambda i: lax.rem(gx + i + gx_n, gx_n)
    wrap_y = lambda i: lax.rem(gy + i + gy_n, gy_n)

    def f_copy(c):
        return pltpu.make_async_copy(flow.at[c], f_buf.at[c], sem_f.at[c])

    def h_copy(c):
        return pltpu.make_async_copy(hist.at[c], h_buf.at[c], sem_h.at[c])

    small = [
        pltpu.make_async_copy(a, b, sem_i.at[i])
        for i, (a, b) in enumerate(
            (
                (cell, i_cell), (shift, i_shift), (frac, i_frac), (speed, i_speed),
                (slots, i_slots), (counts, i_counts),
            )
        )
    ]
    for c in range(6):
        f_copy(c).start()
    for cp in small:
        cp.start()
    for c in range(3):
        h_copy(c).start()

    barrier = pltpu.get_barrier_semaphore()
    for dx, dy in neighbours:
        pl.semaphore_signal(barrier, inc=1, device_id=(wrap_x(dx), wrap_y(dy)), device_id_type=MESH)
    ys[...] = jnp.zeros_like(ys)

    def y_copy(src, dst, sem_s, sem_r, side):
        return pltpu.make_async_remote_copy(
            src_ref=src.at[side], dst_ref=dst.at[1 - side], send_sem=sem_s.at[side],
            recv_sem=sem_r.at[1 - side], device_id=(gx, wrap_y(2 * side - 1)), device_id_type=MESH,
        )

    def pack_x(c, _):
        f_copy(c).wait()
        for z in range(nz):
            sx[0, c, 2 * z : 2 * z + 2, :] = f_buf[c, z, 0:2, :]
            sx[1, c, 2 * z : 2 * z + 2, :] = f_buf[c, z, nx - 2 : nx, :]
        return 0

    lax.fori_loop(0, 6, pack_x, 0)
    def weights(cells, shifts, fracs):
        base = cells + shifts
        w = basis_rows(fracs - shifts.astype(F32))

        def along(pos, dim):
            d = pos - base[dim : dim + 1] + 1
            if dim == 2:
                d = jnp.where(d < 0, d + nz, jnp.where(d >= nz, d - nz, d))
            return pick_weight(d, [v[dim : dim + 1] for v in w])

        return along

    def build_w(w3, width, along):
        wx = along(iota((nx, width), 0), 0)
        wz = along(iota((nz, width), 0), 2)
        for z in range(nz):
            hi, lo = split(wx * wz[z : z + 1])
            w3[z * nx : (z + 1) * nx] = hi
            w3[zx + z * nx : zx + (z + 1) * nx] = hi
            w3[2 * zx + z * nx : 2 * zx + (z + 1) * nx] = lo
        r = iota((xh, width), 0)
        far = r >= half
        q = jnp.where(far, r - half, r)
        hi, lo = split(along(jnp.where(far, nx, -2) + (q & 1), 0) * along(q >> 1, 2))
        w3[k3 : k3 + xh] = hi
        w3[k3 + xh : k3 + 2 * xh] = hi
        w3[k3 + 2 * xh : k3 + 3 * xh] = lo
        w3[k3 + 3 * xh : k3 + 4 * xh] = jnp.zeros_like(lo)

    def product(lo_row, hi_row, w3):
        return jnp.dot(a3[lo_row:hi_row, :], w3[...], preferred_element_type=F32)

    def inner_sum(p, width, along):
        wy = along(iota((ny, width), 0), 1)
        return jnp.sum(p.reshape(6, ny, width) * wy[None], axis=1)

    def outer_sum(p, along):
        wyh = [along(y, 1) for y in (-2, -1, ny, ny + 1)]
        outer = []
        for c in range(6):
            at = 2 * c
            extra = p[at : at + 1] * wyh[0] + p[at + 1 : at + 2] * wyh[1]
            at += 16
            outer.append(extra + p[at : at + 1] * wyh[2] + p[at + 1 : at + 2] * wyh[3])
        return jnp.concatenate(outer, axis=0)

    def interpolate(w3, width, along):
        p = product(0, m + 32, w3)
        return inner_sum(p[0:m], width, along) + outer_sum(p[m:], along)

    def advance(fluid, v0, fracs, tail):
        fluid_u = fluid[0:3]
        fluid_a = fluid[3:6]

        def rate(v):
            return 3.0 * fluid_a + (fluid_u - v) / relax_tau + basset_coef * (fluid_u - v + tail)

        v1 = v0 + step_dt * rate(v0)
        v2 = 0.75 * v0 + 0.25 * (v1 + step_dt * rate(v1))
        vn = v0 / 3.0 + 2.0 / 3.0 * (v2 + step_dt * rate(v2))
        posn = fracs + step_dt * (v0 / 6.0 + v1 / 6.0 + 2.0 * v2 / 3.0)
        return vn, posn, fluid_u - vn

    for c in range(6):
        t = jnp.transpose(f_buf[c].reshape(zx, ny))
        hi, lo = split(t)
        rows = slice(c * ny, (c + 1) * ny)
        a3[rows, 0:zx] = hi
        a3[rows, zx : 2 * zx] = lo
        a3[rows, 2 * zx : 3 * zx] = hi
        pair = slice(2 * (c % 2), 2 * (c % 2) + 2)
        sy[0, c // 2, pair, :] = t[0:2]
        sy[1, c // 2, pair, :] = t[ny - 2 : ny]
    pl.semaphore_wait(barrier, 8)
    x_copies = [
        pltpu.make_async_remote_copy(
            src_ref=sx.at[side], dst_ref=rx.at[1 - side], send_sem=sem_xs.at[side],
            recv_sem=sem_xr.at[1 - side], device_id=(wrap_x(2 * side - 1), gy), device_id_type=MESH,
        )
        for side in range(2)
    ]
    for cp in x_copies:
        cp.start()

    y_copies = [y_copy(sy, ry, sem_ys, sem_yr, side) for side in range(2)]
    for cp in y_copies:
        cp.start()

    for cp in small:
        cp.wait()

    mslot[...] = jnp.zeros_like(mslot)
    mslot[0:8, 0:cap] = i_slots[0].astype(F32)
    cols_t = jnp.transpose(mslot[...])
    for d in range(8):
        col = cols_t[0:cap, d : d + 1]
        col = jnp.where(iota((cap, 1), 0) < i_counts[0, d], col, -1.0).astype(jnp.int32)
        sel[d * cap : (d + 1) * cap, :] = (iota((cap, nb), 1) == col).astype(F32).astype(BF16)
    karg = iota((steps, 128), 0).astype(F32) + 1.0
    quad = (jnp.sqrt(karg + 1.0) - jnp.sqrt(karg))[:, 0:1]

    alive = iota((1, nb), 1) < live[0]
    for c in range(3):
        h_copy(c).wait()
    for c in range(3):
        h = h_buf[c]
        tail_s[c] = jnp.sum(h * quad, axis=0, keepdims=True)
        hi, lo = split(h)
        hhi[c] = hi
        hlo[c] = lo
        picked = contract_lanes(sel[...], hhi[c]) + contract_lanes(sel[...], hlo[c])
        picked = pltpu.roll(picked, 1, 1)
        s_hist[:, :, c * steps : (c + 1) * steps] = picked.reshape(8, cap, steps)
        moved[c] = jnp.where(alive, pltpu.roll(h, 1, 0), 0.0)
    r_copies = [
        pltpu.make_async_remote_copy(
            src_ref=s_hist.at[d], dst_ref=rec_hist.at[d], send_sem=sem_rs.at[d],
            recv_sem=sem_rr.at[d], device_id=(wrap_x(dx), wrap_y(dy)), device_id_type=MESH,
        )
        for d, (dx, dy) in enumerate(neighbours)
    ]
    for cp in r_copies:
        cp.start()

    leaving = 8 * cap
    tail = jnp.concatenate([tail_s[c] for c in range(3)], axis=0)
    own = jnp.concatenate(
        [
            i_cell[...].astype(F32), i_shift[...].astype(F32), i_frac[...], i_speed[...], tail,
            jnp.ones((1, nb), F32),
        ],
        axis=0,
    )
    hi, lo = split(own)
    own = contract_lanes(hi, sel[...]) + contract_lanes(lo, sel[...])
    lv_along = weights(own[0:3].astype(jnp.int32), own[3:6].astype(jnp.int32), own[6:9])
    build_w(w_lv, leaving, lv_along)

    chunks = nb // chunk
    spans = [slice(j * chunk, (j + 1) * chunk) for j in range(chunks)]
    along = [weights(i_cell[:, g], i_shift[:, g], i_frac[:, g]) for g in spans]
    build_w(w3.at[0], chunk, along[0])
    for j in range(1, chunks):
        build_w(w3.at[j], chunk, along[j])
    for cp in x_copies:
        cp.wait()

    for c in range(6):
        block = jnp.concatenate([rx[0, c], rx[1, c], jnp.zeros((ny - xh, ny), F32)], axis=0)
        t = jnp.transpose(block)
        pair = slice(2 * (c % 2), 2 * (c % 2) + 2)
        sc[0, c // 2, pair, :] = t[0:2]
        sc[1, c // 2, pair, :] = t[ny - 2 : ny]
        hi = t.astype(BF16).astype(F32)
        lo = t - hi
        rows = slice(c * ny, (c + 1) * ny)
        a3[rows, k3 : k3 + ny] = (hi + pltpu.roll(lo, xh, 1)).astype(BF16)
        a3[rows, k3 + ny : k3 + 2 * ny] = hi.astype(BF16)
    c_copies = [y_copy(sc, rc, sem_cs, sem_cr, side) for side in range(2)]
    for cp in c_copies:
        cp.start()

    fl[0:6, spans[0]] = inner_sum(product(0, m, w3.at[0]), chunk, along[0])

    for cp in y_copies + c_copies:
        cp.wait()
    for side in range(2):
        rows = slice(m + 16 * side, m + 16 * side + 16)
        for g in range(3):
            ys[side, 4 * g : 4 * g + 4, 0:zx] = ry[side, g]
            ys[side, 4 * g : 4 * g + 4, zx : zx + ny] = rc[side, g]
        v = ys[side]
        hi, lo = split(v[:, 0:zx])
        a3[rows, 0:zx] = hi
        a3[rows, zx : 2 * zx] = lo
        a3[rows, 2 * zx : 3 * zx] = hi
        t = v[:, zx : zx + ny]
        thi = t.astype(BF16).astype(F32)
        a3[rows, k3 : k3 + ny] = (thi + pltpu.roll(t - thi, xh, 1)).astype(BF16)
        a3[rows, k3 + ny : k3 + 2 * ny] = thi.astype(BF16)

    lv = advance(interpolate(w_lv, leaving, lv_along), own[9:12], own[6:9], own[12:15])
    used = own[15:16] > 0.5
    mslot[...] = jnp.zeros_like(mslot)
    for i, v in enumerate(lv):
        mslot[3 * i : 3 * i + 3, :] = jnp.where(used, v, 0.0)
    s_state[...] = jnp.transpose(mslot[...]).reshape(8, cap, 128)
    s_copies = [
        pltpu.make_async_remote_copy(
            src_ref=s_state.at[d], dst_ref=rec_state.at[d], send_sem=sem_ss.at[d],
            recv_sem=sem_sr.at[d], device_id=(wrap_x(dx), wrap_y(dy)), device_id_type=MESH,
        )
        for d, (dx, dy) in enumerate(neighbours)
    ]
    for cp in s_copies:
        cp.start()

    fl[0:6, spans[0]] += outer_sum(product(m, m + 32, w3.at[0]), along[0])
    for j in range(1, chunks):
        fl[0:6, spans[j]] = interpolate(w3.at[j], chunk, along[j])

    keep = iota((3, nb), 1) < live[0]
    for i, v in enumerate(advance(fl[0:6, :], i_speed[...], i_frac[...], tail)):
        res[3 * i : 3 * i + 3, :] = jnp.where(keep, v, 0.0)
    res[9:16, :] = jnp.zeros((7, nb), F32)

    for c in range(3):
        moved[c, 0:1, :] = res[6 + c : 7 + c, :]
    for cp in r_copies + s_copies:
        cp.wait()


def finish_kernel(
    cap, steps,
    res, rec_hist, rec_state, moved,
    vn, posn, out_hist, arr_state, arr_hist,
    b_vn, b_posn, b_state, b_hist, sems,
):
    copies = [pltpu.make_async_copy(moved, out_hist, sems.at[0])]
    copies[0].start()

    def send(src, dst):
        cp = pltpu.make_async_copy(src, dst, sems.at[len(copies)])
        cp.start()
        copies.append(cp)

    b_vn[...] = res[0:3, :]
    send(b_vn, vn)
    b_posn[...] = res[3:6, :]
    send(b_posn, posn)
    t = jnp.transpose(rec_state[...].reshape(8 * cap, 128))
    for d in range(8):
        b_state[:, d, :] = t[0:6, d * cap : (d + 1) * cap]
    send(b_state, arr_state)
    first = iota((cap, steps), 1) == 0
    for d in range(8):
        for c in range(3):
            col = rec_state[d, :, 6 + c : 7 + c]
            b_hist[d, c] = jnp.where(first, col, rec_hist[d, :, c * steps : (c + 1) * steps])
    send(b_hist, arr_hist)
    for cp in copies:
        cp.wait()


def on_device(flow, cell, shift, frac, speed, hist, live, slots, counts):
    _, nz, nx, ny = flow.shape
    nb = speed.shape[1]
    steps = hist.shape[1]
    cap = slots.shape[2]
    zx = nz * nx
    k3 = 3 * zx + 4 * 4 * nz
    chunk = 512
    sizes = (nx, ny, nz, nb, cap, steps, chunk, lax.axis_size("gx"), lax.axis_size("gy"))
    vmem = pl.BlockSpec(memory_space=pltpu.VMEM)
    hbm = pl.BlockSpec(memory_space=pltpu.HBM)
    dma = pltpu.SemaphoreType.DMA
    I32 = jnp.int32
    inputs = (counts, slots, cell, shift, frac, speed, flow, hist)
    gathered = pl.pallas_call(
        functools.partial(main_kernel, sizes),
        out_shape=(
            jax.ShapeDtypeStruct((16, nb), F32),
            jax.ShapeDtypeStruct((8, cap, 3 * steps), F32),
            jax.ShapeDtypeStruct((8, cap, 128), F32),
            jax.ShapeDtypeStruct((3, steps, nb), F32),
        ),
        in_specs=[pl.BlockSpec(memory_space=pltpu.SMEM)] + [hbm] * 8,
        out_specs=[vmem] * 4,
        scratch_shapes=[
            pltpu.VMEM((3, nb), I32),
            pltpu.VMEM((3, nb), I32),
            pltpu.VMEM((3, nb), F32),
            pltpu.VMEM((3, nb), F32),
            pltpu.VMEM((1, 8, cap), I32),
            pltpu.SMEM((1, 8), I32),
            pltpu.VMEM((6, nz, nx, ny), F32),
            pltpu.VMEM((3, steps, nb), F32),
            pltpu.VMEM((6 * ny + 32, k3), BF16),
            pltpu.VMEM((k3, 8 * cap), BF16),
            pltpu.VMEM((nb // chunk, k3, chunk), BF16),
            pltpu.VMEM((2, 6, 2 * nz, ny), F32),
            pltpu.VMEM((2, 6, 2 * nz, ny), F32),
            pltpu.VMEM((2, 3, 4, zx), F32),
            pltpu.VMEM((2, 3, 4, zx), F32),
            pltpu.VMEM((2, 3, 4, ny), F32),
            pltpu.VMEM((2, 3, 4, ny), F32),
            pltpu.VMEM((2, 16, zx + ny), F32),
            pltpu.VMEM((8, nb), F32),
            pltpu.VMEM((8 * cap, nb), BF16),
            pltpu.VMEM((128, 128), F32),
            pltpu.VMEM((3, steps, nb), BF16),
            pltpu.VMEM((3, steps, nb), BF16),
            pltpu.VMEM((3, 1, nb), F32),
            pltpu.VMEM((8, cap, 3 * steps), F32),
            pltpu.VMEM((8, cap, 128), F32),
            dma((6,)), dma((6,)), dma((3,)), dma((2,)), dma((2,)), dma((2,)), dma((2,)),
            dma((2,)), dma((2,)),
            dma((8,)), dma((8,)), dma((8,)), dma((8,)),
        ],
        compiler_params=pltpu.CompilerParams(
            collective_id=0, has_side_effects=True, vmem_limit_bytes=44 * 2**20
        ),
        name="interpolate_and_migrate",
    )(live, *(pltpu.with_memory_space_constraint(v, pltpu.HBM) for v in inputs))

    vn, posn, out_hist, arr_state, arr_hist = pl.pallas_call(
        functools.partial(finish_kernel, cap, steps),
        out_shape=(
            jax.ShapeDtypeStruct((3, nb), F32),
            jax.ShapeDtypeStruct((3, nb), F32),
            jax.ShapeDtypeStruct((3, steps, nb), F32),
            jax.ShapeDtypeStruct((6, 8, cap), F32),
            jax.ShapeDtypeStruct((8, 3, cap, steps), F32),
        ),
        in_specs=[vmem] * 4,
        out_specs=[hbm] * 5,
        scratch_shapes=[
            pltpu.VMEM((3, nb), F32),
            pltpu.VMEM((3, nb), F32),
            pltpu.VMEM((6, 8, cap), F32),
            pltpu.VMEM((8, 3, cap, steps), F32),
            dma((5,)),
        ],
        compiler_params=pltpu.CompilerParams(vmem_limit_bytes=32 * 2**20),
        name="write_results",
    )(*gathered)
    return (
        vn,
        posn,
        out_hist,
        jnp.transpose(arr_state, (1, 0, 2)),
        jnp.transpose(arr_hist, (0, 1, 3, 2)),
    )


def solution(mesh):
    placed = (
        P(None, None, "gx", "gy"),
        P(None, ("gx", "gy")),
        P(None, ("gx", "gy")),
        P(None, ("gx", "gy")),
        P(None, ("gx", "gy")),
        P(None, None, ("gx", "gy")),
        P(("gx", "gy")),
        P(("gx", "gy"), None, None),
        P(("gx", "gy"), None),
    )
    return jax.shard_map(
        on_device,
        mesh=mesh,
        in_specs=placed,
        out_specs=(
            P(None, ("gx", "gy")),
            P(None, ("gx", "gy")),
            P(None, None, ("gx", "gy")),
            P(None, None, ("gx", "gy")),
            P(None, None, None, ("gx", "gy")),
        ),
        check_vma=False,
    )
```

```python
import functools

import jax
import jax.numpy as jnp
from jax import lax
from jax.experimental import pallas as pl
from jax.experimental.pallas import tpu as pltpu
from jax.sharding import PartitionSpec as P

neighbours = ((-1, -1), (-1, 0), (-1, 1), (0, -1), (0, 1), (1, -1), (1, 0), (1, 1))
step_dt = 0.1
relax_tau = 0.5
basset_coef = 0.3
MESH = pl.DeviceIdType.MESH
F32 = jnp.float32
BF16 = jnp.bfloat16


def basis_rows(s):
    return (
        -s * (s - 1.0) * (s - 2.0) / 6.0,
        (s + 1.0) * (s - 1.0) * (s - 2.0) / 2.0,
        -(s + 1.0) * s * (s - 2.0) / 2.0,
        (s + 1.0) * s * (s - 1.0) / 6.0,
    )


def pick_weight(d, w):
    out = jnp.where(d == 0, w[0], 0.0)
    for p in range(1, 4):
        out = jnp.where(d == p, w[p], out)
    return out


def split(v):
    hi = v.astype(BF16)
    return hi, (v - hi.astype(F32)).astype(BF16)


def iota(shape, dim):
    return lax.broadcasted_iota(jnp.int32, shape, dim)


def contract_lanes(a, b):
    return lax.dot_general(a, b, (((1,), (1,)), ((), ())), preferred_element_type=F32)


def main_kernel(
    sizes,
    live, counts, slots, cell, shift, frac, speed, flow, hist,
    res, rec_hist, rec_state, moved,
    i_cell, i_shift, i_frac, i_speed, i_slots, i_counts,
    f_buf, h_buf, a3, w_lv, w3, sx, rx, sy, ry, sc, rc, ys, fl, sel, mslot, hhi, hlo, tail_s, s_hist, s_state,
    sem_i, sem_f, sem_h, sem_xs, sem_xr, sem_ys, sem_yr, sem_cs, sem_cr, sem_rs, sem_rr, sem_ss, sem_sr,
):
    nx, ny, nz, nb, cap, steps, chunk, gx_n, gy_n = sizes
    zx = nz * nx
    xh = 4 * nz
    half = 2 * nz
    k3 = 3 * zx
    m = 6 * ny
    gx = lax.axis_index("gx")
    gy = lax.axis_index("gy")
    wrap_x = lambda i: lax.rem(gx + i + gx_n, gx_n)
    wrap_y = lambda i: lax.rem(gy + i + gy_n, gy_n)

    def f_copy(c):
        return pltpu.make_async_copy(flow.at[c], f_buf.at[c], sem_f.at[c])

    def h_copy(c):
        return pltpu.make_async_copy(hist.at[c], h_buf.at[c], sem_h.at[c])

    small = [
        pltpu.make_async_copy(a, b, sem_i.at[i])
        for i, (a, b) in enumerate(
            (
                (cell, i_cell), (shift, i_shift), (frac, i_frac), (speed, i_speed),
                (slots, i_slots), (counts, i_counts),
            )
        )
    ]
    for c in range(6):
        f_copy(c).start()
    for cp in small:
        cp.start()
    for c in range(3):
        h_copy(c).start()

    barrier = pltpu.get_barrier_semaphore()
    for dx, dy in neighbours:
        pl.semaphore_signal(barrier, inc=1, device_id=(wrap_x(dx), wrap_y(dy)), device_id_type=MESH)
    ys[...] = jnp.zeros_like(ys)

    def y_copy(src, dst, sem_s, sem_r, side):
        return pltpu.make_async_remote_copy(
            src_ref=src.at[side], dst_ref=dst.at[1 - side], send_sem=sem_s.at[side],
            recv_sem=sem_r.at[1 - side], device_id=(gx, wrap_y(2 * side - 1)), device_id_type=MESH,
        )

    def pack_x(c, _):
        f_copy(c).wait()
        for z in range(nz):
            sx[0, c, 2 * z : 2 * z + 2, :] = f_buf[c, z, 0:2, :]
            sx[1, c, 2 * z : 2 * z + 2, :] = f_buf[c, z, nx - 2 : nx, :]
        return 0

    lax.fori_loop(0, 6, pack_x, 0)
    pl.semaphore_wait(barrier, 8)
    x_copies = [
        pltpu.make_async_remote_copy(
            src_ref=sx.at[side], dst_ref=rx.at[1 - side], send_sem=sem_xs.at[side],
            recv_sem=sem_xr.at[1 - side], device_id=(wrap_x(2 * side - 1), gy), device_id_type=MESH,
        )
        for side in range(2)
    ]
    for cp in x_copies:
        cp.start()

    def weights(cells, shifts, fracs):
        base = cells + shifts
        w = basis_rows(fracs - shifts.astype(F32))

        def along(pos, dim):
            d = pos - base[dim : dim + 1] + 1
            if dim == 2:
                d = jnp.where(d < 0, d + nz, jnp.where(d >= nz, d - nz, d))
            return pick_weight(d, [v[dim : dim + 1] for v in w])

        return along

    def build_w(w3, width, along):
        wx = along(iota((nx, width), 0), 0)
        wz = along(iota((nz, width), 0), 2)
        for z in range(nz):
            hi, lo = split(wx * wz[z : z + 1])
            w3[z * nx : (z + 1) * nx] = hi
            w3[zx + z * nx : zx + (z + 1) * nx] = hi
            w3[2 * zx + z * nx : 2 * zx + (z + 1) * nx] = lo
        r = iota((xh, width), 0)
        far = r >= half
        q = jnp.where(far, r - half, r)
        hi, lo = split(along(jnp.where(far, nx, -2) + (q & 1), 0) * along(q >> 1, 2))
        w3[k3 : k3 + xh] = hi
        w3[k3 + xh : k3 + 2 * xh] = hi
        w3[k3 + 2 * xh : k3 + 3 * xh] = lo
        w3[k3 + 3 * xh : k3 + 4 * xh] = jnp.zeros_like(lo)

    def product(lo_row, hi_row, w3):
        return jnp.dot(a3[lo_row:hi_row, :], w3[...], preferred_element_type=F32)

    def inner_sum(p, width, along):
        wy = along(iota((ny, width), 0), 1)
        return jnp.sum(p.reshape(6, ny, width) * wy[None], axis=1)

    def outer_sum(p, along):
        wyh = [along(y, 1) for y in (-2, -1, ny, ny + 1)]
        outer = []
        for c in range(6):
            at = 2 * c
            extra = p[at : at + 1] * wyh[0] + p[at + 1 : at + 2] * wyh[1]
            at += 16
            outer.append(extra + p[at : at + 1] * wyh[2] + p[at + 1 : at + 2] * wyh[3])
        return jnp.concatenate(outer, axis=0)

    def interpolate(w3, width, along):
        p = product(0, m + 32, w3)
        return inner_sum(p[0:m], width, along) + outer_sum(p[m:], along)

    def advance(fluid, v0, fracs, tail):
        fluid_u = fluid[0:3]
        fluid_a = fluid[3:6]

        def rate(v):
            return 3.0 * fluid_a + (fluid_u - v) / relax_tau + basset_coef * (fluid_u - v + tail)

        v1 = v0 + step_dt * rate(v0)
        v2 = 0.75 * v0 + 0.25 * (v1 + step_dt * rate(v1))
        vn = v0 / 3.0 + 2.0 / 3.0 * (v2 + step_dt * rate(v2))
        posn = fracs + step_dt * (v0 / 6.0 + v1 / 6.0 + 2.0 * v2 / 3.0)
        return vn, posn, fluid_u - vn

    for c in range(6):
        t = jnp.transpose(f_buf[c].reshape(zx, ny))
        hi, lo = split(t)
        rows = slice(c * ny, (c + 1) * ny)
        a3[rows, 0:zx] = hi
        a3[rows, zx : 2 * zx] = lo
        a3[rows, 2 * zx : 3 * zx] = hi
        pair = slice(2 * (c % 2), 2 * (c % 2) + 2)
        sy[0, c // 2, pair, :] = t[0:2]
        sy[1, c // 2, pair, :] = t[ny - 2 : ny]
    y_copies = [y_copy(sy, ry, sem_ys, sem_yr, side) for side in range(2)]
    for cp in y_copies:
        cp.start()

    for cp in small:
        cp.wait()

    mslot[...] = jnp.zeros_like(mslot)
    mslot[0:8, 0:cap] = i_slots[0].astype(F32)
    cols_t = jnp.transpose(mslot[...])
    for d in range(8):
        col = cols_t[0:cap, d : d + 1]
        col = jnp.where(iota((cap, 1), 0) < i_counts[0, d], col, -1.0).astype(jnp.int32)
        sel[d * cap : (d + 1) * cap, :] = (iota((cap, nb), 1) == col).astype(F32).astype(BF16)
    karg = iota((steps, 128), 0).astype(F32) + 1.0
    quad = (jnp.sqrt(karg + 1.0) - jnp.sqrt(karg))[:, 0:1]

    alive = iota((1, nb), 1) < live[0]
    for c in range(3):
        h_copy(c).wait()
    for c in range(3):
        h = h_buf[c]
        tail_s[c] = jnp.sum(h * quad, axis=0, keepdims=True)
        hi, lo = split(h)
        hhi[c] = hi
        hlo[c] = lo
        picked = contract_lanes(sel[...], hhi[c]) + contract_lanes(sel[...], hlo[c])
        picked = pltpu.roll(picked, 1, 1)
        s_hist[:, :, c * steps : (c + 1) * steps] = picked.reshape(8, cap, steps)
        moved[c] = jnp.where(alive, pltpu.roll(h, 1, 0), 0.0)
    for cp in x_copies:
        cp.wait()

    for c in range(6):
        block = jnp.concatenate([rx[0, c], rx[1, c], jnp.zeros((ny - xh, ny), F32)], axis=0)
        t = jnp.transpose(block)
        pair = slice(2 * (c % 2), 2 * (c % 2) + 2)
        sc[0, c // 2, pair, :] = t[0:2]
        sc[1, c // 2, pair, :] = t[ny - 2 : ny]
        hi = t.astype(BF16).astype(F32)
        lo = t - hi
        rows = slice(c * ny, (c + 1) * ny)
        a3[rows, k3 : k3 + ny] = (hi + pltpu.roll(lo, xh, 1)).astype(BF16)
        a3[rows, k3 + ny : k3 + 2 * ny] = hi.astype(BF16)
    c_copies = [y_copy(sc, rc, sem_cs, sem_cr, side) for side in range(2)]
    for cp in c_copies:
        cp.start()

    r_copies = [
        pltpu.make_async_remote_copy(
            src_ref=s_hist.at[d], dst_ref=rec_hist.at[d], send_sem=sem_rs.at[d],
            recv_sem=sem_rr.at[d], device_id=(wrap_x(dx), wrap_y(dy)), device_id_type=MESH,
        )
        for d, (dx, dy) in enumerate(neighbours)
    ]
    for cp in r_copies:
        cp.start()

    leaving = 8 * cap
    tail = jnp.concatenate([tail_s[c] for c in range(3)], axis=0)
    own = jnp.concatenate(
        [
            i_cell[...].astype(F32), i_shift[...].astype(F32), i_frac[...], i_speed[...], tail,
            jnp.ones((1, nb), F32),
        ],
        axis=0,
    )
    hi, lo = split(own)
    own = contract_lanes(hi, sel[...]) + contract_lanes(lo, sel[...])
    lv_along = weights(own[0:3].astype(jnp.int32), own[3:6].astype(jnp.int32), own[6:9])
    build_w(w_lv, leaving, lv_along)

    chunks = nb // chunk
    spans = [slice(j * chunk, (j + 1) * chunk) for j in range(chunks)]
    along = [weights(i_cell[:, g], i_shift[:, g], i_frac[:, g]) for g in spans]
    build_w(w3.at[0], chunk, along[0])
    for j in range(1, chunks):
        build_w(w3.at[j], chunk, along[j])
    fl[0:6, spans[0]] = inner_sum(product(0, m, w3.at[0]), chunk, along[0])

    for cp in y_copies + c_copies:
        cp.wait()
    for side in range(2):
        rows = slice(m + 16 * side, m + 16 * side + 16)
        for g in range(3):
            ys[side, 4 * g : 4 * g + 4, 0:zx] = ry[side, g]
            ys[side, 4 * g : 4 * g + 4, zx : zx + ny] = rc[side, g]
        v = ys[side]
        hi, lo = split(v[:, 0:zx])
        a3[rows, 0:zx] = hi
        a3[rows, zx : 2 * zx] = lo
        a3[rows, 2 * zx : 3 * zx] = hi
        t = v[:, zx : zx + ny]
        thi = t.astype(BF16).astype(F32)
        a3[rows, k3 : k3 + ny] = (thi + pltpu.roll(t - thi, xh, 1)).astype(BF16)
        a3[rows, k3 + ny : k3 + 2 * ny] = thi.astype(BF16)

    lv = advance(interpolate(w_lv, leaving, lv_along), own[9:12], own[6:9], own[12:15])
    used = own[15:16] > 0.5
    mslot[...] = jnp.zeros_like(mslot)
    for i, v in enumerate(lv):
        mslot[3 * i : 3 * i + 3, :] = jnp.where(used, v, 0.0)
    s_state[...] = jnp.transpose(mslot[...]).reshape(8, cap, 128)
    s_copies = [
        pltpu.make_async_remote_copy(
            src_ref=s_state.at[d], dst_ref=rec_state.at[d], send_sem=sem_ss.at[d],
            recv_sem=sem_sr.at[d], device_id=(wrap_x(dx), wrap_y(dy)), device_id_type=MESH,
        )
        for d, (dx, dy) in enumerate(neighbours)
    ]
    for cp in s_copies:
        cp.start()

    fl[0:6, spans[0]] += outer_sum(product(m, m + 32, w3.at[0]), along[0])
    for j in range(1, chunks):
        fl[0:6, spans[j]] = interpolate(w3.at[j], chunk, along[j])

    keep = iota((3, nb), 1) < live[0]
    for i, v in enumerate(advance(fl[0:6, :], i_speed[...], i_frac[...], tail)):
        res[3 * i : 3 * i + 3, :] = jnp.where(keep, v, 0.0)
    res[9:16, :] = jnp.zeros((7, nb), F32)

    for c in range(3):
        moved[c, 0:1, :] = res[6 + c : 7 + c, :]
    for cp in r_copies + s_copies:
        cp.wait()


def finish_kernel(
    cap, steps,
    res, rec_hist, rec_state, moved,
    vn, posn, out_hist, arr_state, arr_hist,
    b_vn, b_posn, b_state, b_hist, sems,
):
    copies = [pltpu.make_async_copy(moved, out_hist, sems.at[0])]
    copies[0].start()

    def send(src, dst):
        cp = pltpu.make_async_copy(src, dst, sems.at[len(copies)])
        cp.start()
        copies.append(cp)

    b_vn[...] = res[0:3, :]
    send(b_vn, vn)
    b_posn[...] = res[3:6, :]
    send(b_posn, posn)
    t = jnp.transpose(rec_state[...].reshape(8 * cap, 128))
    for d in range(8):
        b_state[:, d, :] = t[0:6, d * cap : (d + 1) * cap]
    send(b_state, arr_state)
    first = iota((cap, steps), 1) == 0
    for d in range(8):
        for c in range(3):
            col = rec_state[d, :, 6 + c : 7 + c]
            b_hist[d, c] = jnp.where(first, col, rec_hist[d, :, c * steps : (c + 1) * steps])
    send(b_hist, arr_hist)
    for cp in copies:
        cp.wait()


def on_device(flow, cell, shift, frac, speed, hist, live, slots, counts):
    _, nz, nx, ny = flow.shape
    nb = speed.shape[1]
    steps = hist.shape[1]
    cap = slots.shape[2]
    zx = nz * nx
    k3 = 3 * zx + 4 * 4 * nz
    chunk = 512
    sizes = (nx, ny, nz, nb, cap, steps, chunk, lax.axis_size("gx"), lax.axis_size("gy"))
    vmem = pl.BlockSpec(memory_space=pltpu.VMEM)
    hbm = pl.BlockSpec(memory_space=pltpu.HBM)
    dma = pltpu.SemaphoreType.DMA
    I32 = jnp.int32
    inputs = (counts, slots, cell, shift, frac, speed, flow, hist)
    gathered = pl.pallas_call(
        functools.partial(main_kernel, sizes),
        out_shape=(
            jax.ShapeDtypeStruct((16, nb), F32),
            jax.ShapeDtypeStruct((8, cap, 3 * steps), F32),
            jax.ShapeDtypeStruct((8, cap, 128), F32),
            jax.ShapeDtypeStruct((3, steps, nb), F32),
        ),
        in_specs=[pl.BlockSpec(memory_space=pltpu.SMEM)] + [hbm] * 8,
        out_specs=[vmem] * 4,
        scratch_shapes=[
            pltpu.VMEM((3, nb), I32),
            pltpu.VMEM((3, nb), I32),
            pltpu.VMEM((3, nb), F32),
            pltpu.VMEM((3, nb), F32),
            pltpu.VMEM((1, 8, cap), I32),
            pltpu.SMEM((1, 8), I32),
            pltpu.VMEM((6, nz, nx, ny), F32),
            pltpu.VMEM((3, steps, nb), F32),
            pltpu.VMEM((6 * ny + 32, k3), BF16),
            pltpu.VMEM((k3, 8 * cap), BF16),
            pltpu.VMEM((nb // chunk, k3, chunk), BF16),
            pltpu.VMEM((2, 6, 2 * nz, ny), F32),
            pltpu.VMEM((2, 6, 2 * nz, ny), F32),
            pltpu.VMEM((2, 3, 4, zx), F32),
            pltpu.VMEM((2, 3, 4, zx), F32),
            pltpu.VMEM((2, 3, 4, ny), F32),
            pltpu.VMEM((2, 3, 4, ny), F32),
            pltpu.VMEM((2, 16, zx + ny), F32),
            pltpu.VMEM((8, nb), F32),
            pltpu.VMEM((8 * cap, nb), BF16),
            pltpu.VMEM((128, 128), F32),
            pltpu.VMEM((3, steps, nb), BF16),
            pltpu.VMEM((3, steps, nb), BF16),
            pltpu.VMEM((3, 1, nb), F32),
            pltpu.VMEM((8, cap, 3 * steps), F32),
            pltpu.VMEM((8, cap, 128), F32),
            dma((6,)), dma((6,)), dma((3,)), dma((2,)), dma((2,)), dma((2,)), dma((2,)),
            dma((2,)), dma((2,)),
            dma((8,)), dma((8,)), dma((8,)), dma((8,)),
        ],
        compiler_params=pltpu.CompilerParams(
            collective_id=0, has_side_effects=True, vmem_limit_bytes=44 * 2**20
        ),
        name="interpolate_and_migrate",
    )(live, *(pltpu.with_memory_space_constraint(v, pltpu.HBM) for v in inputs))

    vn, posn, out_hist, arr_state, arr_hist = pl.pallas_call(
        functools.partial(finish_kernel, cap, steps),
        out_shape=(
            jax.ShapeDtypeStruct((3, nb), F32),
            jax.ShapeDtypeStruct((3, nb), F32),
            jax.ShapeDtypeStruct((3, steps, nb), F32),
            jax.ShapeDtypeStruct((6, 8, cap), F32),
            jax.ShapeDtypeStruct((8, 3, cap, steps), F32),
        ),
        in_specs=[vmem] * 4,
        out_specs=[hbm] * 5,
        scratch_shapes=[
            pltpu.VMEM((3, nb), F32),
            pltpu.VMEM((3, nb), F32),
            pltpu.VMEM((6, 8, cap), F32),
            pltpu.VMEM((8, 3, cap, steps), F32),
            dma((5,)),
        ],
        compiler_params=pltpu.CompilerParams(vmem_limit_bytes=32 * 2**20),
        name="write_results",
    )(*gathered)
    return (
        vn,
        posn,
        out_hist,
        jnp.transpose(arr_state, (1, 0, 2)),
        jnp.transpose(arr_hist, (0, 1, 3, 2)),
    )


def solution(mesh):
    placed = (
        P(None, None, "gx", "gy"),
        P(None, ("gx", "gy")),
        P(None, ("gx", "gy")),
        P(None, ("gx", "gy")),
        P(None, ("gx", "gy")),
        P(None, None, ("gx", "gy")),
        P(("gx", "gy")),
        P(("gx", "gy"), None, None),
        P(("gx", "gy"), None),
    )
    return jax.shard_map(
        on_device,
        mesh=mesh,
        in_specs=placed,
        out_specs=(
            P(None, ("gx", "gy")),
            P(None, ("gx", "gy")),
            P(None, None, ("gx", "gy")),
            P(None, None, ("gx", "gy")),
            P(None, None, None, ("gx", "gy")),
        ),
        check_vma=False,
    )
```
